32 devices in a mesh: segment: 4 (over z), dp: 8 (over y, x, core).
Axes of the slice: x: 2, y: 2, z: 4, core: 2. Of those that a mesh axis runs over, the one named last changes fastest.
Arguments:
- control_in: bfloat16 [2048, 1536], P('dp'), may hold values from -10 to 10
- base_in: bfloat16 [2048, 2560], P('dp'), may hold values from -6 to 6
- base_update: bfloat16 [4, 2048, 2560], P('segment', 'dp'), may hold values from -4 to 4
- out_gain: float32 [2560], replicated, may hold values from 0.25 to 1.75
- cotangent: bfloat16 [2048, 2560], P('dp'), may hold values from -6 to 6
- w_qkv: bfloat16 [4, 1536, 2304], P('segment', 'dp'), may hold values from -1 to 1
- w_out: bfloat16 [4, 768, 1536], P('segment', 'dp'), may hold values from -0.21875 to 0.21875
- w_hint: bfloat16 [4, 1536, 2560], P('segment', 'dp'), may hold values from -0.15625 to 0.15625
- window_offset: int32 [4, 4], P('segment'), may hold values from -1 to 1
- tile_mask: int32 [4, 4, 4], P('segment'), may hold values 0 or 1
- token_layout: int32 [8, 256], P('dp'), may hold values from 0 to 255, each once within a row
Outputs:
- features: float32 [2048, 2560], P('dp')
- grad_qkv: float32 [4, 1536, 2304], P('segment', 'dp')
- grad_out: float32 [4, 768, 1536], P('segment', 'dp')
- grad_hint: float32 [4, 1536, 2560], P('segment', 'dp')
The draws below stay inside these ranges and needn't reach their ends.
All inputs are finite; a program needn't handle non-finite values. No bound on the sum of `tile_mask` on one device may be relied on, other than what follows from the above.
Results may differ from the reference program's by a relative error of at most 0.03.
Values may be sent and summed in bfloat16 or wider, within the bound.
No kernel may reach another device: no remote copies, remote signals or barrier semaphores. Data moves between devices by JAX's collectives and lax.ppermute only.
A program may use at most 192 MiB of HBM per device.

```python
import jax
import jax.numpy as jnp
from jax import lax

D_CTRL = 1536
HEADS = 6
HEAD = 128
XW = 2560
TILE = 64
TILES = 4
CLIPS_DEV = 1
CLIP_ROWS = 256
CLIPS = 8
TOKENS = 2048
SECTIONS = 4
HD = 768
N_DP = 8


def draw_control_in(key, part):
    key = jax.random.fold_in(key, 11)
    noise_key = jax.random.fold_in(key, 0)
    noise = jnp.clip(jax.random.normal(noise_key, (TOKENS, D_CTRL), jnp.float32), -6.0, 6.0)
    return noise.astype(jnp.bfloat16)


def draw_w_qkv(key, part):
    key = jax.random.fold_in(key, 23)
    base_key = jax.random.fold_in(key, 0)
    weights = jnp.clip(jax.random.normal(base_key, (SECTIONS, D_CTRL, 3, HEADS, HEAD), jnp.float32), -4.0, 4.0) * D_CTRL ** (-0.5)
    return weights.reshape(SECTIONS, D_CTRL, 3 * HEADS * HEAD).astype(jnp.bfloat16)


def set_ends(values, own_key, smallest, top_value):
    place = [jax.random.randint(jax.random.fold_in(own_key, axis), (), 0, length) for axis, length in enumerate(values.shape)]
    widest = values.shape.index(max(values.shape))
    neighbour = place[:widest] + [(place[widest] + 1) % values.shape[widest]] + place[widest + 1:]
    return values.at[tuple(place)].set(smallest).at[tuple(neighbour)].set(top_value)


def level_of(own_key, dims, cuts, low, high):
    level = 1.0
    for dim, shards_of in cuts:
        draws = jax.random.uniform(jax.random.fold_in(jax.random.fold_in(own_key, 6), dim), (shards_of,), jnp.float32, low / len(cuts), high / len(cuts))
        level = level * jnp.repeat(jnp.exp(draws), dims[dim] // shards_of).reshape((-1,) + (1,) * (len(dims) - 1 - dim))
    return level


def scatter_about(key, extent, scale, bound, cuts=(), kind=jnp.bfloat16):
    factor_of = level_of(key, extent, cuts, -0.22, 0.18) if cuts else 1.0
    result = jax.random.normal(key, extent, jnp.float32) * scale * factor_of
    return jnp.minimum(jnp.maximum(result, -bound), bound).astype(kind)


def setup_inputs(seed: int = 0) -> dict:
    streams_of = jax.random.split(jax.random.key(seed), 12)
    control_in = draw_control_in(jax.random.fold_in(streams_of[11], 71), 0)
    base_in = scatter_about(streams_of[1], (TOKENS, XW), 1.0, 6.0, ((0, 8),))
    base_update = scatter_about(streams_of[2], (SECTIONS, TOKENS, XW), 0.5, 4.0, ((0, 4), (1, 8)))
    out_gain = jnp.clip(1.0 + 0.15 * jax.random.normal(streams_of[3], (XW,), jnp.float32), 0.25, 1.75)
    cotangent = scatter_about(streams_of[4], (TOKENS, XW), 1.0, 6.0, ((0, 8),))
    w_qkv = draw_w_qkv(jax.random.fold_in(streams_of[11], 71), 0)
    w_out = scatter_about(streams_of[6], (SECTIONS, HD, D_CTRL), HD ** -0.5, 0.21875, ((0, 4), (1, 8)))
    w_hint = scatter_about(streams_of[7], (SECTIONS, D_CTRL, XW), D_CTRL ** -0.5, 0.15625, ((0, 4), (1, 8)))
    window_offset = set_ends(jax.random.randint(streams_of[8], (SECTIONS, TILES), -1, 2), jax.random.fold_in(streams_of[8], 1), -1, 1).astype(jnp.int32)
    tile_mask = set_ends((jax.random.randint(streams_of[9], (SECTIONS, TILES, TILES), 0, 4) < 3).astype(jnp.int32), jax.random.fold_in(streams_of[9], 1), 0, 1)
    token_layout = jax.vmap(lambda own: jax.random.permutation(own, CLIP_ROWS))(jax.random.split(streams_of[10], CLIPS)).reshape((CLIPS, CLIP_ROWS)).astype(jnp.int32)
    return {"control_in": control_in, "base_in": base_in, "base_update": base_update, "out_gain": out_gain, "cotangent": cotangent, "w_qkv": w_qkv, "w_out": w_out, "w_hint": w_hint, "window_offset": window_offset, "tile_mask": tile_mask, "token_layout": token_layout}


def token_mask(offset, mask):
    count = mask.shape[0]
    row_tile = jnp.arange(count)[:, None]
    col_tile = jnp.arange(count)[None, :]
    near_window = jnp.abs(col_tile - row_tile - offset[:, None]) <= 1
    permitted = (row_tile == col_tile) | near_window & (mask == 1)
    return jnp.repeat(jnp.repeat(permitted, TILE, 0), TILE, 1)

def flat_positions(layout):
    count, length = layout.shape
    return (layout + (jnp.arange(count) * length)[:, None].astype(jnp.int32)).reshape(-1).astype(jnp.int32)

def forward_block(control, positions, permitted, weight_qkv, weight_out, weight_hint):
    total_rows = control.shape[0]
    length = permitted.shape[0]
    count = total_rows // length
    widened = control.astype(jnp.float32)
    inverse = lax.rsqrt(lax.optimization_barrier(jnp.mean(widened * widened, -1, keepdims=True)) + 1e-06)
    normed = (widened * inverse).astype(jnp.bfloat16)
    projected = jnp.dot(normed, weight_qkv, preferred_element_type=jnp.float32).astype(jnp.bfloat16)
    tiled_proj = projected[positions].reshape(count, length, 3, HEADS, HEAD)
    query_rows = tiled_proj[:, :, 0].astype(jnp.float32)
    key_rows = tiled_proj[:, :, 1].astype(jnp.float32)
    value_rows = tiled_proj[:, :, 2].astype(jnp.float32)
    scores = jnp.einsum('cqhe,ckhe->chqk', query_rows, key_rows) * HEAD ** (-0.5)
    scores = jnp.where(permitted, scores, -1e+30)
    row_max = lax.optimization_barrier(jnp.max(scores, -1, keepdims=True))
    shifted = jnp.exp(scores - row_max)
    softmax_out = shifted / lax.optimization_barrier(jnp.sum(shifted, -1, keepdims=True))
    soft_half = softmax_out.astype(jnp.bfloat16)
    attended = jnp.einsum('chqk,ckhe->cqhe', soft_half.astype(jnp.float32), value_rows).astype(jnp.bfloat16)
    attended = attended.reshape(total_rows, HEADS * HEAD)
    merged = jnp.zeros_like(attended).at[positions].set(attended)
    control_out = (widened + jnp.dot(merged, weight_out, preferred_element_type=jnp.float32)).astype(jnp.bfloat16)
    hint_term = jnp.dot(control_out, weight_hint, preferred_element_type=jnp.float32)
    return (control_out, hint_term, (control, normed, tiled_proj, softmax_out, merged))

def backward_block(saved, control_out, grad_next, grad_summed, positions, weight_qkv, weight_out, weight_hint):
    control, normed, tiled_proj, softmax_out, merged = saved
    total_rows = control.shape[0]
    count, length = (tiled_proj.shape[0], tiled_proj.shape[1])
    grad_after = (grad_next.astype(jnp.float32) + jnp.dot(grad_summed, weight_hint.T, preferred_element_type=jnp.float32)).astype(jnp.bfloat16)
    grad_hint = jnp.dot(control_out.T, grad_summed, preferred_element_type=jnp.float32)
    grad_out = jnp.dot(merged.T, grad_after, preferred_element_type=jnp.float32)
    grad_merged = jnp.dot(grad_after, weight_out.T, preferred_element_type=jnp.float32).astype(jnp.bfloat16)
    grad_tiled = grad_merged[positions].reshape(count, length, HEADS, HEAD).astype(jnp.float32)
    query_rows = tiled_proj[:, :, 0].astype(jnp.float32)
    key_rows = tiled_proj[:, :, 1].astype(jnp.float32)
    value_rows = tiled_proj[:, :, 2].astype(jnp.float32)
    soft_half = softmax_out.astype(jnp.bfloat16).astype(jnp.float32)
    grad_values = jnp.einsum('chqk,cqhe->ckhe', soft_half, grad_tiled).astype(jnp.bfloat16)
    grad_probs = jnp.einsum('cqhe,ckhe->chqk', grad_tiled, value_rows)
    grad_scores = softmax_out * (grad_probs - lax.optimization_barrier(jnp.sum(grad_probs * softmax_out, -1, keepdims=True))) * HEAD ** (-0.5)
    grad_scores = grad_scores.astype(jnp.bfloat16).astype(jnp.float32)
    grad_queries = jnp.einsum('chqk,ckhe->cqhe', grad_scores, key_rows).astype(jnp.bfloat16)
    grad_keys = jnp.einsum('chqk,cqhe->ckhe', grad_scores, query_rows).astype(jnp.bfloat16)
    grad_stack = jnp.stack((grad_queries, grad_keys, grad_values), 2).reshape(total_rows, 3 * HEADS * HEAD)
    grad_proj = jnp.zeros_like(grad_stack).at[positions].set(grad_stack)
    grad_qkv = jnp.dot(normed.T, grad_proj, preferred_element_type=jnp.float32)
    grad_normed = jnp.dot(grad_proj, weight_qkv.T, preferred_element_type=jnp.float32)
    widened = control.astype(jnp.float32)
    inverse = lax.rsqrt(lax.optimization_barrier(jnp.mean(widened * widened, -1, keepdims=True)) + 1e-06)
    through = inverse * grad_normed - widened * inverse ** 3 * lax.optimization_barrier(jnp.mean(grad_normed * widened, -1, keepdims=True))
    grad_control = (grad_after.astype(jnp.float32) + through).astype(jnp.bfloat16)
    return (grad_control, (grad_qkv, grad_out, grad_hint))

def norm_grad(summed, gain, cotangent):
    inverse = lax.rsqrt(lax.optimization_barrier(jnp.mean(summed * summed, -1, keepdims=True)) + 1e-06)
    features = summed * inverse * gain
    grad_normed = cotangent.astype(jnp.float32) * gain
    grad_summed = inverse * grad_normed - summed * inverse ** 3 * lax.optimization_barrier(jnp.mean(grad_normed * summed, -1, keepdims=True))
    return (features, grad_summed.astype(jnp.bfloat16))

def reference(control_in, base_in, base_update, out_gain, cotangent, w_qkv, w_out, w_hint, window_offset, tile_mask, token_layout):
    rows_group = CLIPS_DEV * TILES * TILE
    masks = [token_mask(window_offset[section], tile_mask[section]) for section in range(SECTIONS)]
    control_all = control_in.reshape(N_DP, rows_group, D_CTRL)
    base_all = base_in.reshape(N_DP, rows_group, XW)
    update_all = base_update.reshape(SECTIONS, N_DP, rows_group, XW).transpose(1, 0, 2, 3)
    cot_all = cotangent.reshape(N_DP, rows_group, XW)
    layout_all = token_layout.reshape(N_DP, CLIPS_DEV, TILES * TILE)

    def one_group(carry, pieces):
        control, base_rows, updates, cot_rows, layout = pieces
        positions = flat_positions(layout)
        running = jnp.zeros((rows_group, XW), jnp.float32)
        stored = []
        for section in range(SECTIONS):
            control_out, hint_term, saved = forward_block(control, positions, masks[section], w_qkv[section], w_out[section], w_hint[section])
            term = updates[section].astype(jnp.float32) + hint_term
            running = running + term
            stored.append((saved, control_out))
            control = control_out
        summed = base_rows.astype(jnp.float32) + running
        features, grad_summed = norm_grad(summed, out_gain, cot_rows)
        grad_next = jnp.zeros((rows_group, D_CTRL), jnp.bfloat16)
        parts = [None] * SECTIONS
        for section in reversed(range(SECTIONS)):
            saved, control_out = stored[section]
            grad_next, parts[section] = backward_block(saved, control_out, grad_next, grad_summed, positions, w_qkv[section], w_out[section], w_hint[section])
        added = tuple((carry[idx] + jnp.stack([parts[section][idx] for section in range(SECTIONS)]).astype(jnp.bfloat16).astype(jnp.float32) for idx in range(3)))
        return (added, features)
    start = (jnp.zeros(w_qkv.shape, jnp.float32), jnp.zeros(w_out.shape, jnp.float32), jnp.zeros(w_hint.shape, jnp.float32))
    totals, features = lax.scan(one_group, start, (control_all, base_all, update_all, cot_all, layout_all))
    factor = float(TOKENS) ** (-0.5)
    return (features.reshape(N_DP * rows_group, XW), totals[0] * factor, totals[1] * factor, totals[2] * factor)
```

```python
import functools

import jax
import jax.numpy as jnp
from jax import lax
from jax.experimental import pallas as pl
from jax.experimental.pallas import tpu as pltpu
from jax.sharding import PartitionSpec as P

HEADS = 6
HEAD = 128
TILE = 64
HD = HEADS * HEAD
SCALE = HEAD ** (-0.5)
BF = jnp.bfloat16
F32 = jnp.float32
ANY = pl.BlockSpec(memory_space=pl.ANY)
HBM = pl.BlockSpec(memory_space=pltpu.HBM)
SMEM = pl.BlockSpec(memory_space=pltpu.SMEM)
MIB = 1024 * 1024
SECTION_VMEM = 56 * MIB
LAND_VMEM = 46 * MIB
NO_COST = pl.CostEstimate(flops=0, bytes_accessed=0, transcendentals=0)


def mm(a, b):
    return jnp.dot(a, b, preferred_element_type=F32)


def mm_bt(a, b):
    return lax.dot_general(a, b, (((1,), (1,)), ((), ())), preferred_element_type=F32)


def mm_at(a, b):
    return lax.dot_general(a, b, (((0,), (0,)), ((), ())), preferred_element_type=F32)


def token_bias(offset, mask, layout):
    count = mask.shape[0]
    length = layout.shape[0]
    row_tile = jnp.arange(count)[:, None]
    col_tile = jnp.arange(count)[None, :]
    near_window = jnp.abs(col_tile - row_tile - offset[:, None]) <= 1
    permitted = ((row_tile == col_tile) | near_window & (mask == 1)).astype(F32)
    tile_of_position = jnp.arange(length) // TILE
    placed = layout[None, :] == jnp.arange(length)[:, None]
    tile_of_token = jnp.sum(jnp.where(placed, tile_of_position[None, :], 0), 1)
    member = (tile_of_token[:, None] == jnp.arange(count)[None, :]).astype(F32)
    pairs = jnp.dot(jnp.dot(member, permitted), member.T)
    return jnp.where(pairs > 0.5, 0.0, -1e30).astype(F32)


def out_pieces(out_rows):
    main, rest = (2 * out_rows // 3, out_rows // 3)
    return (
        (0, main, 0, 0, 0, 2 * HD),
        (main, rest, 0, 0, 2 * HD, HD),
        (main, rest, HD, rest, 2 * HD, HD),
    )


def pack_kernel(qkv, out, packed, sems):
    qkv_rows, out_rows = (qkv.shape[0], out.shape[0])
    copies = [pltpu.make_async_copy(qkv, packed.at[pl.ds(0, qkv_rows)], sems.at[0])]
    for i, (row, rows, col, prow, pcol, cols) in enumerate(out_pieces(out_rows)):
        copies.append(
            pltpu.make_async_copy(
                out.at[pl.ds(row, rows), pl.ds(col, cols)],
                packed.at[pl.ds(qkv_rows + prow, rows), pl.ds(pcol, cols)],
                sems.at[1 + i],
            )
        )
    for copy in copies:
        copy.start()
    for copy in copies:
        copy.wait()


def pack_shard(qkv, out):
    rows = qkv.shape[0] + out.size // qkv.shape[1]
    return pl.pallas_call(
        pack_kernel,
        out_shape=jax.ShapeDtypeStruct((rows, qkv.shape[1]), BF),
        in_specs=[ANY] * 2,
        out_specs=ANY,
        scratch_shapes=[pltpu.SemaphoreType.DMA((4,))],
        compiler_params=pltpu.CompilerParams(vmem_limit_bytes=MIB),
    )(qkv, out)


def phase_bits(bits, core):
    order = list(range(1, bits + 1))
    return order if core == 0 else order[::-1]


def phase_pairs(bits, phase):
    size = lax.axis_size("dp")
    return [(d, d ^ (1 << phase_bits(bits, d % 2)[phase])) for d in range(size)]


def sibling(value):
    size = lax.axis_size("dp")
    return lax.ppermute(value, "dp", [(d, d ^ 1) for d in range(size)])


def gather_shards(shard, bits, beside):
    held, others = ({0: shard}, {})
    for crossed in range(1, bits + 1):
        near = [p for p in held if p.bit_count() == crossed - 1]
        places = [p for p in range(1 << bits) if p.bit_count() == crossed]
        arrived = []
        for p in places:
            phase = p.bit_length() - 1
            arrived.append(lax.ppermute(held[p ^ (1 << phase)], "dp", phase_pairs(bits, phase)))
        swapped = [sibling(held[p]) for p in near]
        arrived, swapped, beside = lax.optimization_barrier((arrived, swapped, beside))
        held.update(zip(places, arrived))
        others.update(zip(near, swapped))
    others[(1 << bits) - 1] = sibling(held[(1 << bits) - 1])
    flips = [
        [
            sum(1 << bit for i, bit in enumerate(phase_bits(bits, core)) if p >> i & 1)
            for p in range(1 << bits)
        ]
        for core in (0, 1)
    ]
    tables = [flips[core] + [1 ^ f for f in flips[1 - core]] for core in (0, 1)]
    mine = lax.axis_index("dp")
    owners = mine ^ jnp.where(mine % 2 == 0, jnp.array(tables[0]), jnp.array(tables[1]))
    order = range(1 << bits)
    shards = [held[p] for p in order] + [others[p] for p in order]
    return shards, owners.astype(jnp.int32), beside


def land_kernel(first, count, owners, *refs):
    packed, (qkv, out, sems) = (refs[:count], refs[-3:])
    cols = qkv.shape[1]
    total_rows = packed[0].shape[0]
    shards = owners.shape[0]
    qkv_rows, out_rows = (qkv.shape[0] // shards, out.shape[0] // shards)
    for i, ref in enumerate(packed):
        owner = owners[first + i]
        start = pl.multiple_of(owner * qkv_rows, 16)
        pltpu.make_async_copy(
            ref.at[pl.ds(0, qkv_rows)], qkv.at[pl.ds(start, qkv_rows)], sems.at[i]
        ).start()
        for row, rows, col, prow, pcol, width in out_pieces(out_rows):
            start = pl.multiple_of(owner * out_rows + row, 16)
            pltpu.make_async_copy(
                ref.at[pl.ds(qkv_rows + prow, rows), pl.ds(pcol, width)],
                out.at[pl.ds(start, rows), pl.ds(col, width)],
                sems.at[i],
            ).start()
    for i, ref in enumerate(packed):
        pltpu.make_async_copy(ref, ref, sems.at[i]).wait()


def land_shards(owners, packed, first, landed, shapes):
    count = len(packed)
    return pl.pallas_call(
        functools.partial(land_kernel, first, count),
        out_shape=[jax.ShapeDtypeStruct(shape, BF) for shape in shapes],
        in_specs=[SMEM] + [ANY] * (count + len(landed)),
        out_specs=[ANY] * 2,
        input_output_aliases={1 + count + i: i for i in range(len(landed))},
        scratch_shapes=[pltpu.SemaphoreType.DMA((count,))],
        compiler_params=pltpu.CompilerParams(vmem_limit_bytes=SECTION_VMEM if landed else LAND_VMEM),
    )(owners, *packed, *landed)


def nothing_kernel(*refs):
    pass


def unwritten(*shapes):
    return pl.pallas_call(
        nothing_kernel,
        out_shape=[jax.ShapeDtypeStruct(shape, kind) for shape, kind in shapes],
        out_specs=[ANY] * len(shapes),
        compiler_params=pltpu.CompilerParams(vmem_limit_bytes=SECTION_VMEM),
    )()


class SectionWeights:
    def __init__(self, qkv, out, qkv_buf, out_buf, sems):
        self.thirds = [
            pltpu.make_async_copy(qkv.at[:, pl.ds(j * HD, HD)], qkv_buf.at[j], sems.at[j])
            for j in range(3)
        ]
        self.out = pltpu.make_async_copy(out, out_buf, sems.at[3])


def call(kernel, outs, out_specs, scratch, args, specs, aliases):
    return pl.pallas_call(
        kernel,
        out_shape=outs,
        in_specs=specs,
        out_specs=out_specs,
        scratch_shapes=scratch,
        input_output_aliases=aliases,
        compiler_params=pltpu.CompilerParams(vmem_limit_bytes=SECTION_VMEM),
        cost_estimate=NO_COST,
    )(*args)


def forward_kernel(deps, flag, x, bias, w_qkv, w_out, *refs):
    refs = refs[6 + deps :]
    outs, bufs, sems, wsems = (refs[:7], refs[7:-2], refs[-2], refs[-1])
    normed_o, inv_o, proj_o, probs_o, att_o, ctl_o, send_o = outs
    xv, bv, qkv_buf, out_buf, normed_v, inv_v, proj_v, probs_v, att_v, ctl_v = bufs

    @pl.when(flag[0] == 1)
    def _():
        weights = SectionWeights(w_qkv, w_out, qkv_buf, out_buf, wsems)
        get_x = pltpu.make_async_copy(x, xv, sems.at[0])
        get_b = pltpu.make_async_copy(bias, bv, sems.at[1])
        puts = []

        def put(value, out):
            puts.append(pltpu.make_async_copy(value, out, sems.at[2 + len(puts)]))
            puts[-1].start()

        get_x.start()
        for copy in weights.thirds:
            copy.start()
        get_b.start()
        weights.out.start()
        get_x.wait()
        wide = xv[...].astype(F32)
        inverse = lax.rsqrt(jnp.mean(wide * wide, -1, keepdims=True) + 1e-06)
        inv_v[...] = jnp.broadcast_to(inverse, inv_v.shape)
        normed_v[...] = (wide * inverse).astype(BF)
        put(normed_v, normed_o)
        put(inv_v, inv_o)
        for j in range(3):
            weights.thirds[j].wait()
            proj_v[:, j * HD : (j + 1) * HD] = mm(normed_v[...], qkv_buf[j]).astype(BF)
        put(proj_v, proj_o)
        get_b.wait()
        for h in range(HEADS):
            q = proj_v[:, h * HEAD : (h + 1) * HEAD]
            k = proj_v[:, HD + h * HEAD : HD + (h + 1) * HEAD]
            v = proj_v[:, 2 * HD + h * HEAD : 2 * HD + (h + 1) * HEAD]
            scores = mm_bt(q, k) * SCALE + bv[...]
            shifted = jnp.exp(scores - jnp.max(scores, -1, keepdims=True))
            probs = (shifted / jnp.sum(shifted, -1, keepdims=True)).astype(BF)
            probs_v[h] = probs
            att_v[:, h * HEAD : (h + 1) * HEAD] = mm(probs, v).astype(BF)
        put(probs_v, probs_o)
        put(att_v, att_o)
        weights.out.wait()
        ctl_v[...] = (xv[...].astype(F32) + mm(att_v[...], out_buf[...])).astype(BF)
        put(ctl_v, send_o)
        put(ctl_v, ctl_o)
        for copy in puts:
            copy.wait()


def forward_section(flag, x, weights, bias, state, deps):
    rows, width = x.shape
    scratch = [
        pltpu.VMEM((rows, width), BF),
        pltpu.VMEM(bias.shape, F32),
        pltpu.VMEM((3, width, HD), BF),
        pltpu.VMEM((HD, width), BF),
    ]
    scratch += [pltpu.VMEM(s.shape, s.dtype) for s in state]
    scratch += [pltpu.SemaphoreType.DMA((9,)), pltpu.SemaphoreType.DMA((4,))]
    outs = call(
        functools.partial(forward_kernel, len(deps)),
        [jax.ShapeDtypeStruct(s.shape, s.dtype) for s in (*state, x)],
        [HBM] * 6 + [ANY],
        scratch,
        (flag, x, bias, *weights, *state, *deps),
        [SMEM, ANY] + [HBM] * 9 + [ANY] * len(deps),
        {5 + i: i for i in range(6)},
    )
    return outs[:6], outs[6]


def hint_kernel(deps, flag, update, ctl, weight, *refs):
    upper, lower, uv, cv, wv, ov, sems = refs[deps:]
    chunks, _, cols = wv.shape
    half = upper.shape[0]

    @pl.when(flag[0] == 1)
    def _():
        gets = [
            pltpu.make_async_copy(ctl, cv, sems.at[0]),
            pltpu.make_async_copy(update, uv, sems.at[1]),
        ]
        weights = [
            pltpu.make_async_copy(weight.at[:, pl.ds(i * cols, cols)], wv.at[i], sems.at[2 + i])
            for i in range(chunks)
        ]
        gets[0].start()
        weights[0].start()
        gets[1].start()
        for copy in weights[1:]:
            copy.start()
        for copy in gets:
            copy.wait()
        puts = []
        for i in range(chunks):
            weights[i].wait()
            at = slice(i * cols, (i + 1) * cols)
            ov[:, at] = (uv[:, at].astype(F32) + mm(cv[...], wv[i])).astype(BF)
            for j, out in enumerate((upper, lower)):
                puts.append(
                    pltpu.make_async_copy(
                        ov.at[pl.ds(j * half, half), pl.ds(i * cols, cols)],
                        out.at[:, pl.ds(i * cols, cols)],
                        sems.at[2 + chunks + 2 * i + j],
                    )
                )
                puts[-1].start()
        for copy in puts:
            copy.wait()


def hint_term(flag, update, ctl, weight, deps):
    rows, feat = update.shape
    width = ctl.shape[1]
    chunks = 4
    full = pltpu.VMEM((rows, feat), BF)
    return call(
        functools.partial(hint_kernel, len(deps)),
        [jax.ShapeDtypeStruct((rows // 2, feat), BF)] * 2,
        [ANY, ANY],
        [
            full,
            pltpu.VMEM((rows, width), BF),
            pltpu.VMEM((chunks, width, feat // chunks), BF),
            full,
            pltpu.SemaphoreType.DMA((2 + 3 * chunks,)),
        ],
        (flag, update, ctl, weight, *deps),
        [SMEM] + [HBM] * 3 + [ANY] * len(deps),
        {},
    )


def add_kernel(one, two, out):
    out[...] = (one[...].astype(F32) + two[...].astype(F32)).astype(BF)


def add_rows(one, two):
    return pl.pallas_call(
        add_kernel,
        out_shape=jax.ShapeDtypeStruct(one.shape, BF),
        compiler_params=pltpu.CompilerParams(vmem_limit_bytes=8 * MIB),
        cost_estimate=NO_COST,
    )(one, two)


def top_kernel(deps, flag, upper, lower, cot, gain, weight, *refs):
    feat_o, gsum_o, gctl_o, sv, cv, gv, wv, feat_v, gsum_v, gctl_v, sems = refs[3 + deps :]
    chunks, step, _ = wv.shape
    half = upper.shape[0]

    @pl.when(flag[0] == 1)
    def _():
        gets = [
            pltpu.make_async_copy(upper, sv.at[pl.ds(0, half)], sems.at[0]),
            pltpu.make_async_copy(lower, sv.at[pl.ds(half, half)], sems.at[6 + chunks]),
            pltpu.make_async_copy(cot, cv, sems.at[1]),
            pltpu.make_async_copy(gain, gv, sems.at[2]),
        ]
        weights = [
            pltpu.make_async_copy(weight.at[pl.ds(i * step, step)], wv.at[i], sems.at[6 + i])
            for i in range(chunks)
        ]
        for copy in gets + weights:
            copy.start()
        for copy in gets:
            copy.wait()
        total = sv[...].astype(F32)
        inverse = lax.rsqrt(jnp.mean(total * total, -1, keepdims=True) + 1e-06)
        feat_v[...] = total * inverse * gv[...]
        put_feat = pltpu.make_async_copy(feat_v, feat_o, sems.at[3])
        put_feat.start()
        total = sv[...].astype(F32)
        grad_normed = cv[...].astype(F32) * gv[...]
        mean = jnp.mean(grad_normed * total, -1, keepdims=True)
        gsum_v[...] = (inverse * grad_normed - total * (inverse**3 * mean)).astype(BF)
        put_gsum = pltpu.make_async_copy(gsum_v, gsum_o, sems.at[4])
        put_gsum.start()
        for i in range(chunks):
            weights[i].wait()
            gctl_v[:, i * step : (i + 1) * step] = mm_bt(gsum_v[...], wv[i]).astype(BF)
        put_gctl = pltpu.make_async_copy(gctl_v, gctl_o, sems.at[5])
        put_gctl.start()
        put_gctl.wait()
        put_gsum.wait()
        put_feat.wait()


def top_section(flag, summed, cot, gain, weight, state, deps):
    rows, feat = cot.shape
    width = weight.shape[0]
    chunks = 3
    full = pltpu.VMEM((rows, feat), BF)
    return call(
        functools.partial(top_kernel, len(deps)),
        [jax.ShapeDtypeStruct(s.shape, s.dtype) for s in state],
        [HBM] * 3,
        [
            full,
            full,
            pltpu.VMEM((1, feat), F32),
            pltpu.VMEM((chunks, width // chunks, feat), BF),
        ]
        + [pltpu.VMEM(s.shape, s.dtype) for s in state]
        + [pltpu.SemaphoreType.DMA((7 + chunks,))],
        (flag, *summed, cot, gain, weight, *state, *deps),
        [SMEM, ANY, ANY] + [HBM] * 6 + [ANY] * len(deps),
        {6 + i: i for i in range(3)},
    )


def backward_kernel(has_next, deps, flag, w_qkv, w_out, *refs):
    if has_next:
        grad_next, refs = (refs[0], refs[1:])
    gctl, normed, inv, proj, probs = refs[:5]
    refs = refs[8 + deps :]
    outs, bufs, sems, wsems = (refs[:3], refs[3:-2], refs[-2], refs[-1])
    gprev_o, after_o, gproj_o = outs
    gv, gnv, qkv_buf, out_buf, normed_v, inv_v, proj_v, probs_v, gatt_v, after_v, gproj_v, acc = bufs

    @pl.when(flag[0] == 1)
    def _():
        get_g = pltpu.make_async_copy(gctl, gv, sems.at[0])
        get_n = pltpu.make_async_copy(grad_next, gnv, sems.at[1]) if has_next else None
        get_normed = pltpu.make_async_copy(normed, normed_v, sems.at[2])
        get_inv = pltpu.make_async_copy(inv, inv_v, sems.at[3])
        get_proj = pltpu.make_async_copy(proj, proj_v, sems.at[4])
        get_probs = pltpu.make_async_copy(probs, probs_v, sems.at[5])
        weights = SectionWeights(w_qkv, w_out, qkv_buf, out_buf, wsems)
        get_g.start()
        if has_next:
            get_n.start()
        weights.out.start()
        get_proj.start()
        get_probs.start()
        get_g.wait()
        if has_next:
            get_n.wait()
            after_v[...] = (gnv[...].astype(F32) + gv[...].astype(F32)).astype(BF)
        else:
            after_v[...] = gv[...]
        put_after = pltpu.make_async_copy(after_v, after_o, sems.at[6])
        put_after.start()
        for copy in weights.thirds:
            copy.start()
        get_normed.start()
        get_inv.start()
        weights.out.wait()
        gatt_v[...] = mm_bt(after_v[...], out_buf[...]).astype(BF)
        get_proj.wait()
        get_probs.wait()
        for h in range(HEADS):
            at = [slice(j * HD + h * HEAD, j * HD + (h + 1) * HEAD) for j in range(3)]
            q, k, v = (proj_v[:, a] for a in at)
            grad = gatt_v[:, at[0]]
            half = probs_v[h]
            wide = half.astype(F32)
            gproj_v[:, at[2]] = mm_at(half, grad).astype(BF)
            grad_probs = mm_bt(grad, v)
            spread = grad_probs - jnp.sum(grad_probs * wide, -1, keepdims=True)
            grad_scores = (wide * spread * SCALE).astype(BF)
            gproj_v[:, at[0]] = mm(grad_scores, k).astype(BF)
            gproj_v[:, at[1]] = mm_at(grad_scores, q).astype(BF)
        put_gproj = pltpu.make_async_copy(gproj_v, gproj_o, sems.at[7])
        put_gproj.start()
        for j in range(3):
            weights.thirds[j].wait()
            part = mm_bt(gproj_v[:, j * HD : (j + 1) * HD], qkv_buf[j])
            if j == 0:
                acc[...] = part
            else:
                acc[...] += part
        get_normed.wait()
        get_inv.wait()
        wide = normed_v[...].astype(F32)
        mean = jnp.mean(acc[...] * wide, -1, keepdims=True)
        through = inv_v[:, :1] * (acc[...] - normed_v[...].astype(F32) * mean)
        gv[...] = (after_v[...].astype(F32) + through).astype(BF)
        put_gprev = pltpu.make_async_copy(gv, gprev_o, sems.at[8])
        put_gprev.start()
        put_gprev.wait()
        put_after.wait()
        put_gproj.wait()


def backward_section(flag, grad_next, gctl, weights, saved, state, deps):
    rows, width = gctl.shape
    tail = [] if grad_next is None else [grad_next]
    normed, inv, proj, probs = saved
    args = (flag, *weights, *tail, gctl, normed, inv, proj, probs, *state, *deps)
    first = 8 + len(tail)
    full = pltpu.VMEM((rows, width), BF)
    return call(
        functools.partial(backward_kernel, bool(tail), len(deps)),
        [jax.ShapeDtypeStruct(s.shape, s.dtype) for s in state],
        [ANY, HBM, HBM],
        [
            full,
            full,
            pltpu.VMEM((3, width, HD), BF),
            pltpu.VMEM((HD, width), BF),
            full,
            pltpu.VMEM(inv.shape, F32),
            pltpu.VMEM(proj.shape, BF),
            pltpu.VMEM(probs.shape, BF),
            pltpu.VMEM((rows, HD), BF),
            full,
            pltpu.VMEM(proj.shape, BF),
            pltpu.VMEM((rows, width), F32),
            pltpu.SemaphoreType.DMA((9,)),
            pltpu.SemaphoreType.DMA((4,)),
        ],
        args,
        [SMEM, HBM, HBM] + [ANY] * len(tail) + [HBM] * 5 + [ANY] + [HBM] * 2 + [ANY] * len(deps),
        {first + i: i for i in range(1, len(state))},
    )


def out_value_kernel(att, after, after_sib, norm, gproj, gproj_sib, low, high):
    owners, rows, cols = (low.shape[0] * 2, low.shape[1] // 2, low.shape[2])
    clip = after.shape[0]
    values = slice(2 * HD, 3 * HD)
    out = mm(att[:, :clip], after[...]) + mm(att[:, clip:], after_sib[...])
    value = mm(norm[:, :clip], gproj[:, values]) + mm(norm[:, clip:], gproj_sib[:, values])
    for p in range(owners):
        to, at = ((low, p) if p < owners // 2 else (high, p - owners // 2))
        to[at, :rows] = out[p * rows : (p + 1) * rows].astype(BF)
        first = 2 * p * rows
        to[at, rows:, :HD] = value[first : first + rows].astype(BF)
        to[at, rows:, HD:] = value[first + rows : first + 2 * rows].astype(BF)


def product_kernel(norm, gproj, gproj_sib, low, high):
    owners, rows, cols = (low.shape[0] * 2, low.shape[1], low.shape[2])
    clip = gproj.shape[0]
    for p in range(owners):
        to, at = ((low, p) if p < owners // 2 else (high, p - owners // 2))
        mine = norm[p * rows : (p + 1) * rows, :clip]
        other = norm[p * rows : (p + 1) * rows, clip:]
        total = mm(mine, gproj[:, :cols]) + mm(other, gproj_sib[:, :cols])
        to[at] = total.astype(BF)


def owner_products(kernel, args, owners, rows, cols):
    block = jax.ShapeDtypeStruct((owners // 2, rows, cols), BF)
    return pl.pallas_call(
        kernel,
        out_shape=[block, block],
        compiler_params=pltpu.CompilerParams(vmem_limit_bytes=32 * MIB),
        cost_estimate=NO_COST,
    )(*args)


def after_kernel(upper, lower, done, upper_out, lower_out):
    pass


def held_until(values, done):
    return pl.pallas_call(
        after_kernel,
        out_shape=[jax.ShapeDtypeStruct(v.shape, v.dtype) for v in values],
        in_specs=[ANY] * 3,
        out_specs=[ANY] * 2,
        input_output_aliases={0: 0, 1: 1},
        compiler_params=pltpu.CompilerParams(vmem_limit_bytes=MIB),
    )(*values, done)


def owner_kernel(owners, *refs):
    count = owners.shape[0]
    kinds = len(refs) // 4
    for i in range(kinds):
        factor, sib_factor, out, across = refs[i::kinds]
        clip = factor.shape[0]
        rows = out.shape[0] // count
        across[:, :clip] = factor[...].T
        across[:, clip:] = sib_factor[...].T
        for p in range(count):
            start = pl.multiple_of(owners[p] * rows, 16)
            out[p * rows : (p + 1) * rows, :] = across[pl.ds(start, rows), :]


def owner_blocks(factors, sib_factors, bits):
    mine = lax.axis_index("dp")
    flips = [
        [
            sum(1 << bit for i, bit in enumerate(phase_bits(bits, core)) if p >> (bits - 1 - i) & 1)
            for p in range(1 << bits)
        ]
        for core in (0, 1)
    ]
    owners = mine ^ jnp.where(mine % 2 == 0, jnp.array(flips[0]), jnp.array(flips[1]))
    clip = factors[0].shape[0]
    vmem = pl.BlockSpec(memory_space=pltpu.VMEM)
    return pl.pallas_call(
        owner_kernel,
        out_shape=[jax.ShapeDtypeStruct((f.shape[1] // 2, 2 * clip), BF) for f in factors],
        in_specs=[SMEM] + [vmem] * (2 * len(factors)),
        out_specs=[vmem] * len(factors),
        scratch_shapes=[pltpu.VMEM((f.shape[1], 2 * clip), BF) for f in factors],
        compiler_params=pltpu.CompilerParams(vmem_limit_bytes=16 * MIB),
        cost_estimate=NO_COST,
    )(owners.astype(jnp.int32), *factors, *sib_factors)


def sum_to_owner(low, high, bits, factor):
    for phase in range(bits):
        arrived = lax.ppermute(high, "dp", phase_pairs(bits, phase))
        if phase + 1 == bits:
            return (low[0].astype(F32) + arrived[0].astype(F32)) * factor
        count = low.shape[0] // 2
        high = (low[count:].astype(F32) + arrived[count:].astype(F32)).astype(BF)
        low = (low[:count].astype(F32) + arrived[:count].astype(F32)).astype(BF)


def shards(
    control_in,
    base_in,
    base_update,
    out_gain,
    cotangent,
    w_qkv,
    w_out,
    w_hint,
    window_offset,
    tile_mask,
    token_layout,
):
    segments = lax.axis_size("segment")
    devices = lax.axis_size("dp")
    mine = lax.axis_index("segment")
    rows, width = control_in.shape
    feat = base_in.shape[1]
    qkv_rows, out_rows = (w_qkv.shape[1], w_out.shape[1])
    factor = float(rows * devices) ** (-0.5)
    bits = (devices // 2).bit_length() - 1
    bias = token_bias(window_offset[0], tile_mask[0], token_layout[0])
    packed, owners, bias = gather_shards(pack_shard(w_qkv[0], w_out[0]), bits, bias)
    last = devices // 2 - 1
    hint_shard, packed[last] = lax.optimization_barrier((w_hint[0], packed[last]))
    weight_hint = lax.all_gather(hint_shard, "dp", axis=0, tiled=True)
    shapes = ((devices * qkv_rows, 3 * HD), (devices * out_rows, width))
    weights = land_shards(owners, packed[:-1], 0, [], shapes)
    weights = land_shards(owners, packed[-1:], devices - 1, weights, shapes)
    flags = [jnp.where(mine == t, 1, 0).astype(jnp.int32).reshape(1) for t in range(segments)]

    state = unwritten(
        ((rows, width), BF),
        ((rows, HEAD), F32),
        ((rows, 3 * HD), BF),
        ((HEADS, rows, rows), BF),
        ((rows, HD), BF),
        ((rows, width), BF),
    )
    half = rows // 2
    moving = [base_in[:half], base_in[half:]]
    arriving, deps = (control_in, [])

    def add_term(t, moving, state, after=()):
        terms = hint_term(flags[t], base_update[0], state[5], weight_hint, after)
        return [add_rows(m, term) for m, term in zip(moving, terms)]

    for t in range(segments):
        if t > 1:
            deps = add_term(t - 1, moving, state)
            moving = [lax.ppermute(m, "segment", [(t - 1, t)]) for m in deps]
        state, send = forward_section(flags[t], arriving, weights, bias, state, deps)
        if t + 1 < segments:
            arriving = lax.ppermute(send, "segment", [(t, t + 1)])
        if t == 1:
            sums = add_term(0, moving, state, (arriving,))
            moving = [lax.ppermute(m, "segment", [(0, 1)]) for m in sums]
    summed = add_term(segments - 1, moving, state)
    normed, inv, proj, probs, att, ctl = state

    top = unwritten(((rows, feat), F32), ((rows, feat), BF), ((rows, width), BF))
    back = unwritten(((rows, width), BF), ((rows, width), BF), ((rows, 3 * HD), BF))
    gain = out_gain[None]
    owners = devices // 2
    grad_next, deps = (None, [])
    for t in range(segments):
        s = segments - 1 - t
        below = [lax.ppermute(m, "segment", [(s, s - 1)]) for m in summed] if s else None
        held = []
        if s:
            top = top_section(flags[s], summed, cotangent, gain, weight_hint, top, deps)
        if s == 1:
            top = top_section(flags[0], below, cotangent, gain, weight_hint, top, [])
            hint = owner_products(
                product_kernel, (ctl_rows, top[1], sibling(top[1])), owners, qkv_rows, feat
            )
            held = hint[1:]
        back = backward_section(
            flags[s], grad_next, top[2], weights, (normed, inv, proj, probs), back, held
        )
        deps = [back[2]]
        if s:
            grad_next = lax.ppermute(back[0], "segment", [(s, s - 1)])
        if t == 1:
            factors, _ = lax.optimization_barrier(((normed, att, ctl), back[2]))
            norm_rows, att_rows, ctl_rows = owner_blocks(
                factors, [sibling(f) for f in factors], bits
            )
            deps = [back[2], norm_rows]
        summed = held_until(below, back[1]) if t and s > 1 else below
    _, after, gproj = back
    after_sib, gproj_sib = (sibling(after), sibling(gproj))
    first = owner_products(
        out_value_kernel,
        (att_rows, after, after_sib, norm_rows, gproj, gproj_sib),
        owners,
        2 * out_rows,
        width,
    )
    second = owner_products(
        product_kernel, (norm_rows, gproj, gproj_sib), owners, qkv_rows, 2 * HD
    )
    first = sum_to_owner(*first, bits, factor)
    second = sum_to_owner(*second, bits, factor)
    third = sum_to_owner(*hint, bits, factor)
    value = jnp.concatenate((first[out_rows:, :HD], first[out_rows:, HD:]), 0)
    return (
        top[0],
        jnp.concatenate((second, value), 1)[None],
        first[None, :out_rows],
        third[None],
    )


def solution(mesh):
    placed = (
        P("dp", None),
        P("dp", None),
        P("segment", "dp", None),
        P(),
        P("dp", None),
        P("segment", "dp", None),
        P("segment", "dp", None),
        P("segment", "dp", None),
        P("segment", None),
        P("segment", None, None),
        P("dp", None),
    )
    return jax.shard_map(
        shards,
        mesh=mesh,
        in_specs=placed,
        out_specs=(
            P("dp", None),
            P("segment", "dp", None),
            P("segment", "dp", None),
            P("segment", "dp", None),
        ),
        check_vma=False,
    )
```

```python
import functools

import jax
import jax.numpy as jnp
from jax import lax
from jax.experimental import pallas as pl
from jax.experimental.pallas import tpu as pltpu
from jax.sharding import PartitionSpec as P

HEADS = 6
HEAD = 128
TILE = 64
HD = HEADS * HEAD
SCALE = HEAD ** (-0.5)
BF = jnp.bfloat16
F32 = jnp.float32
ANY = pl.BlockSpec(memory_space=pl.ANY)
HBM = pl.BlockSpec(memory_space=pltpu.HBM)
SMEM = pl.BlockSpec(memory_space=pltpu.SMEM)
MIB = 1024 * 1024
SECTION_VMEM = 56 * MIB
NO_COST = pl.CostEstimate(flops=0, bytes_accessed=0, transcendentals=0)


def mm(a, b):
    return jnp.dot(a, b, preferred_element_type=F32)


def mm_bt(a, b):
    return lax.dot_general(a, b, (((1,), (1,)), ((), ())), preferred_element_type=F32)


def mm_at(a, b):
    return lax.dot_general(a, b, (((0,), (0,)), ((), ())), preferred_element_type=F32)


def token_bias(offset, mask, layout):
    count = mask.shape[0]
    length = layout.shape[0]
    row_tile = jnp.arange(count)[:, None]
    col_tile = jnp.arange(count)[None, :]
    near_window = jnp.abs(col_tile - row_tile - offset[:, None]) <= 1
    permitted = ((row_tile == col_tile) | near_window & (mask == 1)).astype(F32)
    tile_of_position = jnp.arange(length) // TILE
    placed = layout[None, :] == jnp.arange(length)[:, None]
    tile_of_token = jnp.sum(jnp.where(placed, tile_of_position[None, :], 0), 1)
    member = (tile_of_token[:, None] == jnp.arange(count)[None, :]).astype(F32)
    pairs = jnp.dot(jnp.dot(member, permitted), member.T)
    return jnp.where(pairs > 0.5, 0.0, -1e30).astype(F32)


def out_pieces(out_rows):
    main, rest = (2 * out_rows // 3, out_rows // 3)
    return (
        (0, main, 0, 0, 0, 2 * HD),
        (main, rest, 0, 0, 2 * HD, HD),
        (main, rest, HD, rest, 2 * HD, HD),
    )


def pack_kernel(qkv, out, packed, sems):
    qkv_rows, out_rows = (qkv.shape[0], out.shape[0])
    copies = [pltpu.make_async_copy(qkv, packed.at[pl.ds(0, qkv_rows)], sems.at[0])]
    for i, (row, rows, col, prow, pcol, cols) in enumerate(out_pieces(out_rows)):
        copies.append(
            pltpu.make_async_copy(
                out.at[pl.ds(row, rows), pl.ds(col, cols)],
                packed.at[pl.ds(qkv_rows + prow, rows), pl.ds(pcol, cols)],
                sems.at[1 + i],
            )
        )
    for copy in copies:
        copy.start()
    for copy in copies:
        copy.wait()


def pack_shard(qkv, out):
    rows = qkv.shape[0] + out.size // qkv.shape[1]
    return pl.pallas_call(
        pack_kernel,
        out_shape=jax.ShapeDtypeStruct((rows, qkv.shape[1]), BF),
        in_specs=[ANY] * 2,
        out_specs=ANY,
        scratch_shapes=[pltpu.SemaphoreType.DMA((4,))],
        compiler_params=pltpu.CompilerParams(vmem_limit_bytes=MIB),
    )(qkv, out)


def phase_bits(bits, core):
    order = list(range(1, bits + 1))
    return order if core == 0 else order[::-1]


def phase_pairs(bits, phase):
    size = lax.axis_size("dp")
    return [(d, d ^ (1 << phase_bits(bits, d % 2)[phase])) for d in range(size)]


def sibling(value):
    size = lax.axis_size("dp")
    return lax.ppermute(value, "dp", [(d, d ^ 1) for d in range(size)])


def gather_shards(shard, bits, beside):
    held, others = ({0: shard}, {})
    for crossed in range(1, bits + 1):
        near = [p for p in held if p.bit_count() == crossed - 1]
        places = [p for p in range(1 << bits) if p.bit_count() == crossed]
        arrived = []
        for p in places:
            phase = p.bit_length() - 1
            arrived.append(lax.ppermute(held[p ^ (1 << phase)], "dp", phase_pairs(bits, phase)))
        swapped = [sibling(held[p]) for p in near]
        arrived, swapped, beside = lax.optimization_barrier((arrived, swapped, beside))
        held.update(zip(places, arrived))
        others.update(zip(near, swapped))
    others[(1 << bits) - 1] = sibling(held[(1 << bits) - 1])
    flips = [
        [
            sum(1 << bit for i, bit in enumerate(phase_bits(bits, core)) if p >> i & 1)
            for p in range(1 << bits)
        ]
        for core in (0, 1)
    ]
    tables = [flips[core] + [1 ^ f for f in flips[1 - core]] for core in (0, 1)]
    mine = lax.axis_index("dp")
    owners = mine ^ jnp.where(mine % 2 == 0, jnp.array(tables[0]), jnp.array(tables[1]))
    order = range(1 << bits)
    shards = [held[p] for p in order] + [others[p] for p in order]
    return shards, owners.astype(jnp.int32), beside


def nothing_kernel(*refs):
    pass


def unwritten(*shapes):
    return pl.pallas_call(
        nothing_kernel,
        out_shape=[jax.ShapeDtypeStruct(shape, kind) for shape, kind in shapes],
        out_specs=[ANY] * len(shapes),
        compiler_params=pltpu.CompilerParams(vmem_limit_bytes=SECTION_VMEM),
    )()


class SectionWeights:
    def __init__(self, owners, packed, qkv_buf, out_buf, sems):
        self.owners, self.packed, self.sems = (owners, packed, sems)
        self.qkv_buf, self.out_buf = (qkv_buf, out_buf)

    def start_third(self, j):
        rows = self.qkv_buf.shape[2]
        for i, ref in enumerate(self.packed):
            pltpu.make_async_copy(
                ref.at[pl.ds(0, rows), pl.ds(j * HD, HD)],
                self.qkv_buf.at[j, self.owners[i]],
                self.sems.at[j],
            ).start()

    def wait_third(self, j):
        whole = self.qkv_buf.at[j]
        pltpu.make_async_copy(whole, whole, self.sems.at[j]).wait()

    def start_out(self):
        qkv_rows = self.qkv_buf.shape[2]
        out_rows = self.out_buf.shape[0] // len(self.packed)
        for i, ref in enumerate(self.packed):
            for row, rows, col, prow, pcol, cols in out_pieces(out_rows):
                start = pl.multiple_of(self.owners[i] * out_rows + row, 16)
                pltpu.make_async_copy(
                    ref.at[pl.ds(qkv_rows + prow, rows), pl.ds(pcol, cols)],
                    self.out_buf.at[pl.ds(start, rows), pl.ds(col, cols)],
                    self.sems.at[3],
                ).start()

    def wait_out(self):
        pltpu.make_async_copy(self.out_buf, self.out_buf, self.sems.at[3]).wait()


def call(kernel, outs, out_specs, scratch, args, specs, aliases):
    return pl.pallas_call(
        kernel,
        out_shape=outs,
        in_specs=specs,
        out_specs=out_specs,
        scratch_shapes=scratch,
        input_output_aliases=aliases,
        compiler_params=pltpu.CompilerParams(vmem_limit_bytes=SECTION_VMEM),
        cost_estimate=NO_COST,
    )(*args)


def forward_kernel(shards, deps, flag, owners, x, bias, *refs):
    packed, refs = (refs[:shards], refs[shards + 6 + deps :])
    outs, bufs, sems, wsems = (refs[:7], refs[7:-2], refs[-2], refs[-1])
    normed_o, inv_o, proj_o, probs_o, att_o, ctl_o, send_o = outs
    xv, bv, qkv_buf, out_buf, normed_v, inv_v, proj_v, probs_v, att_v, ctl_v = bufs

    @pl.when(flag[0] == 1)
    def _():
        weights = SectionWeights(owners, packed, qkv_buf, out_buf, wsems)
        get_x = pltpu.make_async_copy(x, xv, sems.at[0])
        get_b = pltpu.make_async_copy(bias, bv, sems.at[1])
        puts = []

        def put(value, out):
            puts.append(pltpu.make_async_copy(value, out, sems.at[2 + len(puts)]))
            puts[-1].start()

        get_x.start()
        weights.start_third(0)
        get_x.wait()
        wide = xv[...].astype(F32)
        inverse = lax.rsqrt(jnp.mean(wide * wide, -1, keepdims=True) + 1e-06)
        inv_v[...] = jnp.broadcast_to(inverse, inv_v.shape)
        normed_v[...] = (wide * inverse).astype(BF)
        weights.start_third(1)
        weights.start_third(2)
        get_b.start()
        weights.start_out()
        for j in range(3):
            weights.wait_third(j)
            weight = qkv_buf[j].reshape(-1, HD)
            proj_v[:, j * HD : (j + 1) * HD] = mm(normed_v[...], weight).astype(BF)
        put(normed_v, normed_o)
        put(inv_v, inv_o)
        put(proj_v, proj_o)
        get_b.wait()
        for h in range(HEADS):
            q = proj_v[:, h * HEAD : (h + 1) * HEAD]
            k = proj_v[:, HD + h * HEAD : HD + (h + 1) * HEAD]
            v = proj_v[:, 2 * HD + h * HEAD : 2 * HD + (h + 1) * HEAD]
            scores = mm_bt(q, k) * SCALE + bv[...]
            shifted = jnp.exp(scores - jnp.max(scores, -1, keepdims=True))
            probs = (shifted / jnp.sum(shifted, -1, keepdims=True)).astype(BF)
            probs_v[h] = probs
            att_v[:, h * HEAD : (h + 1) * HEAD] = mm(probs, v).astype(BF)
        put(probs_v, probs_o)
        put(att_v, att_o)
        weights.wait_out()
        ctl_v[...] = (xv[...].astype(F32) + mm(att_v[...], out_buf[...])).astype(BF)
        put(ctl_v, send_o)
        put(ctl_v, ctl_o)
        for copy in puts:
            copy.wait()


def forward_section(flag, x, weights, bias, state, deps):
    rows, width = x.shape
    owners, packed = weights
    shards, qkv_rows = (len(packed), width // len(packed))
    scratch = [
        pltpu.VMEM((rows, width), BF),
        pltpu.VMEM(bias.shape, F32),
        pltpu.VMEM((3, shards, qkv_rows, HD), BF),
        pltpu.VMEM((HD, width), BF),
    ]
    scratch += [pltpu.VMEM(s.shape, s.dtype) for s in state]
    scratch += [pltpu.SemaphoreType.DMA((9,)), pltpu.SemaphoreType.DMA((4,))]
    outs = call(
        functools.partial(forward_kernel, shards, len(deps)),
        [jax.ShapeDtypeStruct(s.shape, s.dtype) for s in (*state, x)],
        [HBM] * 6 + [ANY],
        scratch,
        (flag, owners, x, bias, *packed, *state, *deps),
        [SMEM, SMEM, ANY] + [HBM] * (7 + shards) + [ANY] * len(deps),
        {4 + shards + i: i for i in range(6)},
    )
    return outs[:6], outs[6]


def hint_kernel(deps, flag, update, ctl, weight, *refs):
    upper, lower, uv, cv, wv, ov, sems = refs[deps:]
    chunks, _, cols = wv.shape
    half = upper.shape[0]

    @pl.when(flag[0] == 1)
    def _():
        gets = [
            pltpu.make_async_copy(ctl, cv, sems.at[0]),
            pltpu.make_async_copy(update, uv, sems.at[1]),
        ]
        weights = [
            pltpu.make_async_copy(weight.at[:, pl.ds(i * cols, cols)], wv.at[i], sems.at[2 + i])
            for i in range(chunks)
        ]
        gets[0].start()
        weights[0].start()
        gets[1].start()
        for copy in weights[1:]:
            copy.start()
        for copy in gets:
            copy.wait()
        puts = []
        for i in range(chunks):
            weights[i].wait()
            at = slice(i * cols, (i + 1) * cols)
            ov[:, at] = (uv[:, at].astype(F32) + mm(cv[...], wv[i])).astype(BF)
            for j, out in enumerate((upper, lower)):
                puts.append(
                    pltpu.make_async_copy(
                        ov.at[pl.ds(j * half, half), pl.ds(i * cols, cols)],
                        out.at[:, pl.ds(i * cols, cols)],
                        sems.at[2 + chunks + 2 * i + j],
                    )
                )
                puts[-1].start()
        for copy in puts:
            copy.wait()


def hint_term(flag, update, ctl, weight, deps):
    rows, feat = update.shape
    width = ctl.shape[1]
    chunks = 4
    full = pltpu.VMEM((rows, feat), BF)
    return call(
        functools.partial(hint_kernel, len(deps)),
        [jax.ShapeDtypeStruct((rows // 2, feat), BF)] * 2,
        [ANY, ANY],
        [
            full,
            pltpu.VMEM((rows, width), BF),
            pltpu.VMEM((chunks, width, feat // chunks), BF),
            full,
            pltpu.SemaphoreType.DMA((2 + 3 * chunks,)),
        ],
        (flag, update, ctl, weight, *deps),
        [SMEM] + [HBM] * 3 + [ANY] * len(deps),
        {},
    )


def add_kernel(one, two, out):
    out[...] = (one[...].astype(F32) + two[...].astype(F32)).astype(BF)


def add_rows(one, two):
    return pl.pallas_call(
        add_kernel,
        out_shape=jax.ShapeDtypeStruct(one.shape, BF),
        compiler_params=pltpu.CompilerParams(vmem_limit_bytes=8 * MIB),
        cost_estimate=NO_COST,
    )(one, two)


def top_kernel(deps, flag, upper, lower, cot, gain, weight, *refs):
    feat_o, gsum_o, gctl_o, sv, cv, gv, wv, feat_v, gsum_v, gctl_v, sems = refs[3 + deps :]
    chunks, step, _ = wv.shape
    half = upper.shape[0]

    @pl.when(flag[0] == 1)
    def _():
        gets = [
            pltpu.make_async_copy(upper, sv.at[pl.ds(0, half)], sems.at[0]),
            pltpu.make_async_copy(lower, sv.at[pl.ds(half, half)], sems.at[6 + chunks]),
            pltpu.make_async_copy(cot, cv, sems.at[1]),
            pltpu.make_async_copy(gain, gv, sems.at[2]),
        ]
        weights = [
            pltpu.make_async_copy(weight.at[pl.ds(i * step, step)], wv.at[i], sems.at[6 + i])
            for i in range(chunks)
        ]
        for copy in gets + weights:
            copy.start()
        for copy in gets:
            copy.wait()
        total = sv[...].astype(F32)
        inverse = lax.rsqrt(jnp.mean(total * total, -1, keepdims=True) + 1e-06)
        feat_v[...] = total * inverse * gv[...]
        put_feat = pltpu.make_async_copy(feat_v, feat_o, sems.at[3])
        put_feat.start()
        total = sv[...].astype(F32)
        grad_normed = cv[...].astype(F32) * gv[...]
        mean = jnp.mean(grad_normed * total, -1, keepdims=True)
        gsum_v[...] = (inverse * grad_normed - total * (inverse**3 * mean)).astype(BF)
        put_gsum = pltpu.make_async_copy(gsum_v, gsum_o, sems.at[4])
        put_gsum.start()
        for i in range(chunks):
            weights[i].wait()
            gctl_v[:, i * step : (i + 1) * step] = mm_bt(gsum_v[...], wv[i]).astype(BF)
        put_gctl = pltpu.make_async_copy(gctl_v, gctl_o, sems.at[5])
        put_gctl.start()
        put_gctl.wait()
        put_gsum.wait()
        put_feat.wait()


def top_section(flag, summed, cot, gain, weight, state, deps):
    rows, feat = cot.shape
    width = weight.shape[0]
    chunks = 3
    full = pltpu.VMEM((rows, feat), BF)
    return call(
        functools.partial(top_kernel, len(deps)),
        [jax.ShapeDtypeStruct(s.shape, s.dtype) for s in state],
        [HBM] * 3,
        [
            full,
            full,
            pltpu.VMEM((1, feat), F32),
            pltpu.VMEM((chunks, width // chunks, feat), BF),
        ]
        + [pltpu.VMEM(s.shape, s.dtype) for s in state]
        + [pltpu.SemaphoreType.DMA((7 + chunks,))],
        (flag, *summed, cot, gain, weight, *state, *deps),
        [SMEM, ANY, ANY] + [HBM] * 6 + [ANY] * len(deps),
        {6 + i: i for i in range(3)},
    )


def backward_kernel(has_next, shards, deps, flag, owners, *refs):
    if has_next:
        grad_next, refs = (refs[0], refs[1:])
    packed, refs = (refs[:shards], refs[shards:])
    gctl, normed, inv, proj, probs = refs[:5]
    refs = refs[8 + deps :]
    outs, bufs, sems, wsems = (refs[:3], refs[3:-2], refs[-2], refs[-1])
    gprev_o, after_o, gproj_o = outs
    gv, gnv, qkv_buf, out_buf, normed_v, inv_v, proj_v, probs_v, gatt_v, after_v, gproj_v, acc = bufs

    @pl.when(flag[0] == 1)
    def _():
        get_g = pltpu.make_async_copy(gctl, gv, sems.at[0])
        get_n = pltpu.make_async_copy(grad_next, gnv, sems.at[1]) if has_next else None
        get_normed = pltpu.make_async_copy(normed, normed_v, sems.at[2])
        get_inv = pltpu.make_async_copy(inv, inv_v, sems.at[3])
        get_proj = pltpu.make_async_copy(proj, proj_v, sems.at[4])
        get_probs = pltpu.make_async_copy(probs, probs_v, sems.at[5])
        weights = SectionWeights(owners, packed, qkv_buf, out_buf, wsems)
        get_g.start()
        if has_next:
            get_n.start()
        weights.start_out()
        get_proj.start()
        get_probs.start()
        get_g.wait()
        if has_next:
            get_n.wait()
            after_v[...] = (gnv[...].astype(F32) + gv[...].astype(F32)).astype(BF)
        else:
            after_v[...] = gv[...]
        put_after = pltpu.make_async_copy(after_v, after_o, sems.at[6])
        put_after.start()
        for j in range(3):
            weights.start_third(j)
        get_normed.start()
        get_inv.start()
        weights.wait_out()
        gatt_v[...] = mm_bt(after_v[...], out_buf[...]).astype(BF)
        get_proj.wait()
        get_probs.wait()
        for h in range(HEADS):
            at = [slice(j * HD + h * HEAD, j * HD + (h + 1) * HEAD) for j in range(3)]
            q, k, v = (proj_v[:, a] for a in at)
            grad = gatt_v[:, at[0]]
            half = probs_v[h]
            wide = half.astype(F32)
            gproj_v[:, at[2]] = mm_at(half, grad).astype(BF)
            grad_probs = mm_bt(grad, v)
            spread = grad_probs - jnp.sum(grad_probs * wide, -1, keepdims=True)
            grad_scores = (wide * spread * SCALE).astype(BF)
            gproj_v[:, at[0]] = mm(grad_scores, k).astype(BF)
            gproj_v[:, at[1]] = mm_at(grad_scores, q).astype(BF)
        put_gproj = pltpu.make_async_copy(gproj_v, gproj_o, sems.at[7])
        put_gproj.start()
        for j in range(3):
            weights.wait_third(j)
            part = mm_bt(gproj_v[:, j * HD : (j + 1) * HD], qkv_buf[j].reshape(-1, HD))
            if j == 0:
                acc[...] = part
            else:
                acc[...] += part
        get_normed.wait()
        get_inv.wait()
        wide = normed_v[...].astype(F32)
        mean = jnp.mean(acc[...] * wide, -1, keepdims=True)
        through = inv_v[:, :1] * (acc[...] - normed_v[...].astype(F32) * mean)
        gv[...] = (after_v[...].astype(F32) + through).astype(BF)
        put_gprev = pltpu.make_async_copy(gv, gprev_o, sems.at[8])
        put_gprev.start()
        put_gprev.wait()
        put_after.wait()
        put_gproj.wait()


def backward_section(flag, grad_next, gctl, weights, saved, state, deps):
    rows, width = gctl.shape
    owners, packed = weights
    shards, qkv_rows = (len(packed), width // len(packed))
    tail = [] if grad_next is None else [grad_next]
    normed, inv, proj, probs = saved
    args = (flag, owners, *tail, *packed, gctl, normed, inv, proj, probs, *state, *deps)
    first = 7 + len(tail) + shards
    full = pltpu.VMEM((rows, width), BF)
    return call(
        functools.partial(backward_kernel, bool(tail), shards, len(deps)),
        [jax.ShapeDtypeStruct(s.shape, s.dtype) for s in state],
        [ANY, HBM, HBM],
        [
            full,
            full,
            pltpu.VMEM((3, shards, qkv_rows, HD), BF),
            pltpu.VMEM((HD, width), BF),
            full,
            pltpu.VMEM(inv.shape, F32),
            pltpu.VMEM(proj.shape, BF),
            pltpu.VMEM(probs.shape, BF),
            pltpu.VMEM((rows, HD), BF),
            full,
            pltpu.VMEM(proj.shape, BF),
            pltpu.VMEM((rows, width), F32),
            pltpu.SemaphoreType.DMA((9,)),
            pltpu.SemaphoreType.DMA((4,)),
        ],
        args,
        [SMEM, SMEM] + [ANY] * len(tail) + [HBM] * (5 + shards) + [ANY] + [HBM] * 2 + [ANY] * len(deps),
        {first + i: i for i in range(1, len(state))},
    )


def out_value_kernel(att, after, after_sib, norm, gproj, gproj_sib, low, high):
    owners, rows, cols = (low.shape[0] * 2, low.shape[1] // 2, low.shape[2])
    clip = after.shape[0]
    values = slice(2 * HD, 3 * HD)
    out = mm(att[:, :clip], after[...]) + mm(att[:, clip:], after_sib[...])
    value = mm(norm[:, :clip], gproj[:, values]) + mm(norm[:, clip:], gproj_sib[:, values])
    for p in range(owners):
        to, at = ((low, p) if p < owners // 2 else (high, p - owners // 2))
        to[at, :rows] = out[p * rows : (p + 1) * rows].astype(BF)
        first = 2 * p * rows
        to[at, rows:, :HD] = value[first : first + rows].astype(BF)
        to[at, rows:, HD:] = value[first + rows : first + 2 * rows].astype(BF)


def product_kernel(norm, gproj, gproj_sib, low, high):
    owners, rows, cols = (low.shape[0] * 2, low.shape[1], low.shape[2])
    clip = gproj.shape[0]
    for p in range(owners):
        to, at = ((low, p) if p < owners // 2 else (high, p - owners // 2))
        mine = norm[p * rows : (p + 1) * rows, :clip]
        other = norm[p * rows : (p + 1) * rows, clip:]
        total = mm(mine, gproj[:, :cols]) + mm(other, gproj_sib[:, :cols])
        to[at] = total.astype(BF)


def owner_products(kernel, args, owners, rows, cols):
    block = jax.ShapeDtypeStruct((owners // 2, rows, cols), BF)
    return pl.pallas_call(
        kernel,
        out_shape=[block, block],
        compiler_params=pltpu.CompilerParams(vmem_limit_bytes=32 * MIB),
        cost_estimate=NO_COST,
    )(*args)


def after_kernel(upper, lower, done, upper_out, lower_out):
    pass


def held_until(values, done):
    return pl.pallas_call(
        after_kernel,
        out_shape=[jax.ShapeDtypeStruct(v.shape, v.dtype) for v in values],
        in_specs=[ANY] * 3,
        out_specs=[ANY] * 2,
        input_output_aliases={0: 0, 1: 1},
        compiler_params=pltpu.CompilerParams(vmem_limit_bytes=MIB),
    )(*values, done)


def owner_kernel(owners, *refs):
    count = owners.shape[0]
    kinds = len(refs) // 4
    for i in range(kinds):
        factor, sib_factor, out, across = refs[i::kinds]
        clip = factor.shape[0]
        rows = out.shape[0] // count
        across[:, :clip] = factor[...].T
        across[:, clip:] = sib_factor[...].T
        for p in range(count):
            start = pl.multiple_of(owners[p] * rows, 16)
            out[p * rows : (p + 1) * rows, :] = across[pl.ds(start, rows), :]


def owner_blocks(factors, sib_factors, bits):
    mine = lax.axis_index("dp")
    flips = [
        [
            sum(1 << bit for i, bit in enumerate(phase_bits(bits, core)) if p >> (bits - 1 - i) & 1)
            for p in range(1 << bits)
        ]
        for core in (0, 1)
    ]
    owners = mine ^ jnp.where(mine % 2 == 0, jnp.array(flips[0]), jnp.array(flips[1]))
    clip = factors[0].shape[0]
    vmem = pl.BlockSpec(memory_space=pltpu.VMEM)
    return pl.pallas_call(
        owner_kernel,
        out_shape=[jax.ShapeDtypeStruct((f.shape[1] // 2, 2 * clip), BF) for f in factors],
        in_specs=[SMEM] + [vmem] * (2 * len(factors)),
        out_specs=[vmem] * len(factors),
        scratch_shapes=[pltpu.VMEM((f.shape[1], 2 * clip), BF) for f in factors],
        compiler_params=pltpu.CompilerParams(vmem_limit_bytes=16 * MIB),
        cost_estimate=NO_COST,
    )(owners.astype(jnp.int32), *factors, *sib_factors)


def sum_to_owner(low, high, bits, factor):
    for phase in range(bits):
        arrived = lax.ppermute(high, "dp", phase_pairs(bits, phase))
        if phase + 1 == bits:
            return (low[0].astype(F32) + arrived[0].astype(F32)) * factor
        count = low.shape[0] // 2
        high = (low[count:].astype(F32) + arrived[count:].astype(F32)).astype(BF)
        low = (low[:count].astype(F32) + arrived[:count].astype(F32)).astype(BF)


def shards(
    control_in,
    base_in,
    base_update,
    out_gain,
    cotangent,
    w_qkv,
    w_out,
    w_hint,
    window_offset,
    tile_mask,
    token_layout,
):
    segments = lax.axis_size("segment")
    devices = lax.axis_size("dp")
    mine = lax.axis_index("segment")
    rows, width = control_in.shape
    feat = base_in.shape[1]
    qkv_rows, out_rows = (w_qkv.shape[1], w_out.shape[1])
    factor = float(rows * devices) ** (-0.5)
    bits = (devices // 2).bit_length() - 1
    bias = token_bias(window_offset[0], tile_mask[0], token_layout[0])
    packed, owners, bias = gather_shards(pack_shard(w_qkv[0], w_out[0]), bits, bias)
    last = devices // 2 - 1
    hint_shard, packed[last] = lax.optimization_barrier((w_hint[0], packed[last]))
    weight_hint = lax.all_gather(hint_shard, "dp", axis=0, tiled=True)
    weights = (owners, packed)
    flags = [jnp.where(mine == t, 1, 0).astype(jnp.int32).reshape(1) for t in range(segments)]

    state = unwritten(
        ((rows, width), BF),
        ((rows, HEAD), F32),
        ((rows, 3 * HD), BF),
        ((HEADS, rows, rows), BF),
        ((rows, HD), BF),
        ((rows, width), BF),
    )
    half = rows // 2
    moving = [base_in[:half], base_in[half:]]
    arriving, deps = (control_in, [])

    def add_term(t, moving, state, after=()):
        terms = hint_term(flags[t], base_update[0], state[5], weight_hint, after)
        return [add_rows(m, term) for m, term in zip(moving, terms)]

    for t in range(segments):
        if t > 1:
            deps = add_term(t - 1, moving, state)
            moving = [lax.ppermute(m, "segment", [(t - 1, t)]) for m in deps]
        state, send = forward_section(flags[t], arriving, weights, bias, state, deps)
        if t + 1 < segments:
            arriving = lax.ppermute(send, "segment", [(t, t + 1)])
        if t == 1:
            sums = add_term(0, moving, state, (arriving,))
            moving = [lax.ppermute(m, "segment", [(0, 1)]) for m in sums]
    summed = add_term(segments - 1, moving, state)
    normed, inv, proj, probs, att, ctl = state

    top = unwritten(((rows, feat), F32), ((rows, feat), BF), ((rows, width), BF))
    back = unwritten(((rows, width), BF), ((rows, width), BF), ((rows, 3 * HD), BF))
    gain = out_gain[None]
    owners = devices // 2
    saved = (normed, inv, proj, probs)
    grad_next, deps = (None, [])
    for t in range(segments):
        s = segments - 1 - t
        held = []
        below = [lax.ppermute(m, "segment", [(s, s - 1)]) for m in summed] if s else None
        if t < segments - 1:
            top = top_section(flags[s], summed, cotangent, gain, weight_hint, top, deps)
        if s == 1:
            deps = [] if grad_next is None else [grad_next]
            top = top_section(flags[0], below, cotangent, gain, weight_hint, top, deps)
            factors, _ = lax.optimization_barrier(((normed, att, ctl), top[1]))
            norm_rows, att_rows, ctl_rows = owner_blocks(
                factors, [sibling(f) for f in factors], bits
            )
            hint = owner_products(
                product_kernel, (ctl_rows, top[1], sibling(top[1])), owners, qkv_rows, feat
            )
        if s == 0:
            held = hint[1:]
        back = backward_section(flags[s], grad_next, top[2], weights, saved, back, held)
        deps = [back[2]]
        if s:
            grad_next = lax.ppermute(back[0], "segment", [(s, s - 1)])
        summed = held_until(below, back[1]) if t and s > 1 else below
    _, after, gproj = back
    after_sib, gproj_sib = (sibling(after), sibling(gproj))
    first = owner_products(
        out_value_kernel,
        (att_rows, after, after_sib, norm_rows, gproj, gproj_sib),
        owners,
        2 * out_rows,
        width,
    )
    second = owner_products(
        product_kernel, (norm_rows, gproj, gproj_sib), owners, qkv_rows, 2 * HD
    )
    first = sum_to_owner(*first, bits, factor)
    second = sum_to_owner(*second, bits, factor)
    third = sum_to_owner(*hint, bits, factor)
    value = jnp.concatenate((first[out_rows:, :HD], first[out_rows:, HD:]), 0)
    return (
        top[0],
        jnp.concatenate((second, value), 1)[None],
        first[None, :out_rows],
        third[None],
    )


def solution(mesh):
    placed = (
        P("dp", None),
        P("dp", None),
        P("segment", "dp", None),
        P(),
        P("dp", None),
        P("segment", "dp", None),
        P("segment", "dp", None),
        P("segment", "dp", None),
        P("segment", None),
        P("segment", None, None),
        P("dp", None),
    )
    return jax.shard_map(
        shards,
        mesh=mesh,
        in_specs=placed,
        out_specs=(
            P("dp", None),
            P("segment", "dp", None),
            P("segment", "dp", None),
            P("segment", "dp", None),
        ),
        check_vma=False,
    )
```

```python
import functools

import jax
import jax.numpy as jnp
from jax import lax
from jax.experimental import pallas as pl
from jax.experimental.pallas import tpu as pltpu
from jax.sharding import PartitionSpec as P

HEADS = 6
HEAD = 128
TILE = 64
HD = HEADS * HEAD
SCALE = HEAD ** (-0.5)
BF = jnp.bfloat16
F32 = jnp.float32
ANY = pl.BlockSpec(memory_space=pl.ANY)
HBM = pl.BlockSpec(memory_space=pltpu.HBM)
SMEM = pl.BlockSpec(memory_space=pltpu.SMEM)
MIB = 1024 * 1024
SECTION_VMEM = 56 * MIB
NO_COST = pl.CostEstimate(flops=0, bytes_accessed=0, transcendentals=0)


def mm(a, b):
    return jnp.dot(a, b, preferred_element_type=F32)


def mm_bt(a, b):
    return lax.dot_general(a, b, (((1,), (1,)), ((), ())), preferred_element_type=F32)


def mm_at(a, b):
    return lax.dot_general(a, b, (((0,), (0,)), ((), ())), preferred_element_type=F32)


def token_bias(offset, mask, layout):
    count = mask.shape[0]
    length = layout.shape[0]
    row_tile = jnp.arange(count)[:, None]
    col_tile = jnp.arange(count)[None, :]
    near_window = jnp.abs(col_tile - row_tile - offset[:, None]) <= 1
    permitted = ((row_tile == col_tile) | near_window & (mask == 1)).astype(F32)
    tile_of_position = jnp.arange(length) // TILE
    placed = layout[None, :] == jnp.arange(length)[:, None]
    tile_of_token = jnp.sum(jnp.where(placed, tile_of_position[None, :], 0), 1)
    member = (tile_of_token[:, None] == jnp.arange(count)[None, :]).astype(F32)
    pairs = jnp.dot(jnp.dot(member, permitted), member.T)
    return jnp.where(pairs > 0.5, 0.0, -1e30).astype(F32)


def out_pieces(out_rows):
    main, rest = (2 * out_rows // 3, out_rows // 3)
    return (
        (0, main, 0, 0, 0, 2 * HD),
        (main, rest, 0, 0, 2 * HD, HD),
        (main, rest, HD, rest, 2 * HD, HD),
    )


def pack_kernel(qkv, out, packed, sems):
    qkv_rows, out_rows = (qkv.shape[0], out.shape[0])
    copies = [pltpu.make_async_copy(qkv, packed.at[pl.ds(0, qkv_rows)], sems.at[0])]
    for i, (row, rows, col, prow, pcol, cols) in enumerate(out_pieces(out_rows)):
        copies.append(
            pltpu.make_async_copy(
                out.at[pl.ds(row, rows), pl.ds(col, cols)],
                packed.at[pl.ds(qkv_rows + prow, rows), pl.ds(pcol, cols)],
                sems.at[1 + i],
            )
        )
    for copy in copies:
        copy.start()
    for copy in copies:
        copy.wait()


def pack_shard(qkv, out):
    rows = qkv.shape[0] + out.size // qkv.shape[1]
    return pl.pallas_call(
        pack_kernel,
        out_shape=jax.ShapeDtypeStruct((rows, qkv.shape[1]), BF),
        in_specs=[ANY] * 2,
        out_specs=ANY,
        scratch_shapes=[pltpu.SemaphoreType.DMA((4,))],
        compiler_params=pltpu.CompilerParams(vmem_limit_bytes=MIB),
    )(qkv, out)


def phase_bits(bits, core):
    order = list(range(1, bits + 1))
    return order if core == 0 else order[::-1]


def phase_pairs(bits, phase):
    size = lax.axis_size("dp")
    return [(d, d ^ (1 << phase_bits(bits, d % 2)[phase])) for d in range(size)]


def sibling(value):
    size = lax.axis_size("dp")
    return lax.ppermute(value, "dp", [(d, d ^ 1) for d in range(size)])


def gather_shards(shard, bits, beside):
    held, others = ({0: shard}, {})
    for crossed in range(1, bits + 1):
        near = [p for p in held if p.bit_count() == crossed - 1]
        places = [p for p in range(1 << bits) if p.bit_count() == crossed]
        arrived = []
        for p in places:
            phase = p.bit_length() - 1
            arrived.append(lax.ppermute(held[p ^ (1 << phase)], "dp", phase_pairs(bits, phase)))
        swapped = [sibling(held[p]) for p in near]
        arrived, swapped, beside = lax.optimization_barrier((arrived, swapped, beside))
        held.update(zip(places, arrived))
        others.update(zip(near, swapped))
    others[(1 << bits) - 1] = sibling(held[(1 << bits) - 1])
    flips = [
        [
            sum(1 << bit for i, bit in enumerate(phase_bits(bits, core)) if p >> i & 1)
            for p in range(1 << bits)
        ]
        for core in (0, 1)
    ]
    tables = [flips[core] + [1 ^ f for f in flips[1 - core]] for core in (0, 1)]
    mine = lax.axis_index("dp")
    owners = mine ^ jnp.where(mine % 2 == 0, jnp.array(tables[0]), jnp.array(tables[1]))
    order = range(1 << bits)
    shards = [held[p] for p in order] + [others[p] for p in order]
    return shards, owners.astype(jnp.int32), beside


def nothing_kernel(*refs):
    pass


def unwritten(*shapes):
    return pl.pallas_call(
        nothing_kernel,
        out_shape=[jax.ShapeDtypeStruct(shape, kind) for shape, kind in shapes],
        out_specs=[ANY] * len(shapes),
        compiler_params=pltpu.CompilerParams(vmem_limit_bytes=SECTION_VMEM),
    )()


class SectionWeights:
    def __init__(self, owners, packed, qkv_buf, out_buf, sems):
        self.owners, self.packed, self.sems = (owners, packed, sems)
        self.qkv_buf, self.out_buf = (qkv_buf, out_buf)

    def start_third(self, j):
        rows = self.qkv_buf.shape[2]
        for i, ref in enumerate(self.packed):
            pltpu.make_async_copy(
                ref.at[pl.ds(0, rows), pl.ds(j * HD, HD)],
                self.qkv_buf.at[j, self.owners[i]],
                self.sems.at[j],
            ).start()

    def wait_third(self, j):
        whole = self.qkv_buf.at[j]
        pltpu.make_async_copy(whole, whole, self.sems.at[j]).wait()

    def start_out(self):
        qkv_rows = self.qkv_buf.shape[2]
        out_rows = self.out_buf.shape[0] // len(self.packed)
        for i, ref in enumerate(self.packed):
            for row, rows, col, prow, pcol, cols in out_pieces(out_rows):
                start = pl.multiple_of(self.owners[i] * out_rows + row, 16)
                pltpu.make_async_copy(
                    ref.at[pl.ds(qkv_rows + prow, rows), pl.ds(pcol, cols)],
                    self.out_buf.at[pl.ds(start, rows), pl.ds(col, cols)],
                    self.sems.at[3],
                ).start()

    def wait_out(self):
        pltpu.make_async_copy(self.out_buf, self.out_buf, self.sems.at[3]).wait()


def call(kernel, outs, out_specs, scratch, args, specs, aliases):
    return pl.pallas_call(
        kernel,
        out_shape=outs,
        in_specs=specs,
        out_specs=out_specs,
        scratch_shapes=scratch,
        input_output_aliases=aliases,
        compiler_params=pltpu.CompilerParams(vmem_limit_bytes=SECTION_VMEM),
        cost_estimate=NO_COST,
    )(*args)


def forward_kernel(shards, deps, flag, owners, x, bias, *refs):
    packed, refs = (refs[:shards], refs[shards + 6 + deps :])
    outs, bufs, sems, wsems = (refs[:7], refs[7:-2], refs[-2], refs[-1])
    normed_o, inv_o, proj_o, probs_o, att_o, ctl_o, send_o = outs
    xv, bv, qkv_buf, out_buf, normed_v, inv_v, proj_v, probs_v, att_v, ctl_v = bufs

    @pl.when(flag[0] == 1)
    def _():
        weights = SectionWeights(owners, packed, qkv_buf, out_buf, wsems)
        get_x = pltpu.make_async_copy(x, xv, sems.at[0])
        get_b = pltpu.make_async_copy(bias, bv, sems.at[1])
        puts = []

        def put(value, out):
            puts.append(pltpu.make_async_copy(value, out, sems.at[2 + len(puts)]))
            puts[-1].start()

        get_x.start()
        weights.start_third(0)
        get_x.wait()
        wide = xv[...].astype(F32)
        inverse = lax.rsqrt(jnp.mean(wide * wide, -1, keepdims=True) + 1e-06)
        inv_v[...] = jnp.broadcast_to(inverse, inv_v.shape)
        normed_v[...] = (wide * inverse).astype(BF)
        weights.start_third(1)
        weights.start_third(2)
        get_b.start()
        weights.start_out()
        for j in range(3):
            weights.wait_third(j)
            weight = qkv_buf[j].reshape(-1, HD)
            proj_v[:, j * HD : (j + 1) * HD] = mm(normed_v[...], weight).astype(BF)
        put(normed_v, normed_o)
        put(inv_v, inv_o)
        put(proj_v, proj_o)
        get_b.wait()
        for h in range(HEADS):
            q = proj_v[:, h * HEAD : (h + 1) * HEAD]
            k = proj_v[:, HD + h * HEAD : HD + (h + 1) * HEAD]
            v = proj_v[:, 2 * HD + h * HEAD : 2 * HD + (h + 1) * HEAD]
            scores = mm_bt(q, k) * SCALE + bv[...]
            shifted = jnp.exp(scores - jnp.max(scores, -1, keepdims=True))
            probs = (shifted / jnp.sum(shifted, -1, keepdims=True)).astype(BF)
            probs_v[h] = probs
            att_v[:, h * HEAD : (h + 1) * HEAD] = mm(probs, v).astype(BF)
        put(probs_v, probs_o)
        put(att_v, att_o)
        weights.wait_out()
        ctl_v[...] = (xv[...].astype(F32) + mm(att_v[...], out_buf[...])).astype(BF)
        put(ctl_v, send_o)
        put(ctl_v, ctl_o)
        for copy in puts:
            copy.wait()


def forward_section(flag, x, weights, bias, state, deps):
    rows, width = x.shape
    owners, packed = weights
    shards, qkv_rows = (len(packed), width // len(packed))
    scratch = [
        pltpu.VMEM((rows, width), BF),
        pltpu.VMEM(bias.shape, F32),
        pltpu.VMEM((3, shards, qkv_rows, HD), BF),
        pltpu.VMEM((HD, width), BF),
    ]
    scratch += [pltpu.VMEM(s.shape, s.dtype) for s in state]
    scratch += [pltpu.SemaphoreType.DMA((9,)), pltpu.SemaphoreType.DMA((4,))]
    outs = call(
        functools.partial(forward_kernel, shards, len(deps)),
        [jax.ShapeDtypeStruct(s.shape, s.dtype) for s in (*state, x)],
        [HBM] * 6 + [ANY],
        scratch,
        (flag, owners, x, bias, *packed, *state, *deps),
        [SMEM, SMEM, ANY] + [HBM] * (7 + shards) + [ANY] * len(deps),
        {4 + shards + i: i for i in range(6)},
    )
    return outs[:6], outs[6]


def hint_kernel(deps, flag, update, ctl, weight, *refs):
    upper, lower, uv, cv, wv, ov, sems = refs[deps:]
    chunks, _, cols = wv.shape
    half = upper.shape[0]

    @pl.when(flag[0] == 1)
    def _():
        gets = [
            pltpu.make_async_copy(ctl, cv, sems.at[0]),
            pltpu.make_async_copy(update, uv, sems.at[1]),
        ]
        weights = [
            pltpu.make_async_copy(weight.at[:, pl.ds(i * cols, cols)], wv.at[i], sems.at[2 + i])
            for i in range(chunks)
        ]
        gets[0].start()
        weights[0].start()
        gets[1].start()
        for copy in weights[1:]:
            copy.start()
        for copy in gets:
            copy.wait()
        puts = []
        for i in range(chunks):
            weights[i].wait()
            at = slice(i * cols, (i + 1) * cols)
            ov[:, at] = (uv[:, at].astype(F32) + mm(cv[...], wv[i])).astype(BF)
            for j, out in enumerate((upper, lower)):
                puts.append(
                    pltpu.make_async_copy(
                        ov.at[pl.ds(j * half, half), pl.ds(i * cols, cols)],
                        out.at[:, pl.ds(i * cols, cols)],
                        sems.at[2 + chunks + 2 * i + j],
                    )
                )
                puts[-1].start()
        for copy in puts:
            copy.wait()


def hint_term(flag, update, ctl, weight, deps):
    rows, feat = update.shape
    width = ctl.shape[1]
    chunks = 4
    full = pltpu.VMEM((rows, feat), BF)
    return call(
        functools.partial(hint_kernel, len(deps)),
        [jax.ShapeDtypeStruct((rows // 2, feat), BF)] * 2,
        [ANY, ANY],
        [
            full,
            pltpu.VMEM((rows, width), BF),
            pltpu.VMEM((chunks, width, feat // chunks), BF),
            full,
            pltpu.SemaphoreType.DMA((2 + 3 * chunks,)),
        ],
        (flag, update, ctl, weight, *deps),
        [SMEM] + [HBM] * 3 + [ANY] * len(deps),
        {},
    )


def add_kernel(one, two, *refs):
    refs[-1][...] = (one[...].astype(F32) + two[...].astype(F32)).astype(BF)


def add_rows(one, two, deps=()):
    vmem = pl.BlockSpec(memory_space=pltpu.VMEM)
    return pl.pallas_call(
        add_kernel,
        out_shape=jax.ShapeDtypeStruct(one.shape, BF),
        in_specs=[vmem, vmem] + [ANY] * len(deps),
        compiler_params=pltpu.CompilerParams(vmem_limit_bytes=8 * MIB),
        cost_estimate=NO_COST,
    )(one, two, *deps)


def top_kernel(deps, flag, upper, lower, cot, gain, weight, *refs):
    feat_o, gsum_o, gctl_o, sv, cv, gv, wv, feat_v, gsum_v, gctl_v, sems = refs[3 + deps :]
    chunks, step, _ = wv.shape
    half = upper.shape[0]

    @pl.when(flag[0] == 1)
    def _():
        gets = [
            pltpu.make_async_copy(upper, sv.at[pl.ds(0, half)], sems.at[0]),
            pltpu.make_async_copy(lower, sv.at[pl.ds(half, half)], sems.at[6 + chunks]),
            pltpu.make_async_copy(cot, cv, sems.at[1]),
            pltpu.make_async_copy(gain, gv, sems.at[2]),
        ]
        weights = [
            pltpu.make_async_copy(weight.at[pl.ds(i * step, step)], wv.at[i], sems.at[6 + i])
            for i in range(chunks)
        ]
        for copy in gets + weights:
            copy.start()
        for copy in gets:
            copy.wait()
        total = sv[...].astype(F32)
        inverse = lax.rsqrt(jnp.mean(total * total, -1, keepdims=True) + 1e-06)
        feat_v[...] = total * inverse * gv[...]
        put_feat = pltpu.make_async_copy(feat_v, feat_o, sems.at[3])
        put_feat.start()
        total = sv[...].astype(F32)
        grad_normed = cv[...].astype(F32) * gv[...]
        mean = jnp.mean(grad_normed * total, -1, keepdims=True)
        gsum_v[...] = (inverse * grad_normed - total * (inverse**3 * mean)).astype(BF)
        put_gsum = pltpu.make_async_copy(gsum_v, gsum_o, sems.at[4])
        put_gsum.start()
        for i in range(chunks):
            weights[i].wait()
            gctl_v[:, i * step : (i + 1) * step] = mm_bt(gsum_v[...], wv[i]).astype(BF)
        put_gctl = pltpu.make_async_copy(gctl_v, gctl_o, sems.at[5])
        put_gctl.start()
        put_gctl.wait()
        put_gsum.wait()
        put_feat.wait()


def top_section(flag, summed, cot, gain, weight, state, deps):
    rows, feat = cot.shape
    width = weight.shape[0]
    chunks = 3
    full = pltpu.VMEM((rows, feat), BF)
    return call(
        functools.partial(top_kernel, len(deps)),
        [jax.ShapeDtypeStruct(s.shape, s.dtype) for s in state],
        [HBM] * 3,
        [
            full,
            full,
            pltpu.VMEM((1, feat), F32),
            pltpu.VMEM((chunks, width // chunks, feat), BF),
        ]
        + [pltpu.VMEM(s.shape, s.dtype) for s in state]
        + [pltpu.SemaphoreType.DMA((7 + chunks,))],
        (flag, *summed, cot, gain, weight, *state, *deps),
        [SMEM, ANY, ANY] + [HBM] * 6 + [ANY] * len(deps),
        {6 + i: i for i in range(3)},
    )


def backward_kernel(has_next, shards, deps, flag, owners, *refs):
    if has_next:
        grad_next, refs = (refs[0], refs[1:])
    packed, refs = (refs[:shards], refs[shards:])
    gctl, normed, inv, proj, probs = refs[:5]
    refs = refs[8 + deps :]
    outs, bufs, sems, wsems = (refs[:3], refs[3:-2], refs[-2], refs[-1])
    gprev_o, after_o, gproj_o = outs
    gv, gnv, qkv_buf, out_buf, normed_v, inv_v, proj_v, probs_v, gatt_v, after_v, gproj_v, acc = bufs

    @pl.when(flag[0] == 1)
    def _():
        get_g = pltpu.make_async_copy(gctl, gv, sems.at[0])
        get_n = pltpu.make_async_copy(grad_next, gnv, sems.at[1]) if has_next else None
        get_normed = pltpu.make_async_copy(normed, normed_v, sems.at[2])
        get_inv = pltpu.make_async_copy(inv, inv_v, sems.at[3])
        get_proj = pltpu.make_async_copy(proj, proj_v, sems.at[4])
        get_probs = pltpu.make_async_copy(probs, probs_v, sems.at[5])
        weights = SectionWeights(owners, packed, qkv_buf, out_buf, wsems)
        get_g.start()
        if has_next:
            get_n.start()
        weights.start_out()
        get_proj.start()
        get_probs.start()
        get_g.wait()
        if has_next:
            get_n.wait()
            after_v[...] = (gnv[...].astype(F32) + gv[...].astype(F32)).astype(BF)
        else:
            after_v[...] = gv[...]
        put_after = pltpu.make_async_copy(after_v, after_o, sems.at[6])
        put_after.start()
        for j in range(3):
            weights.start_third(j)
        get_normed.start()
        get_inv.start()
        weights.wait_out()
        gatt_v[...] = mm_bt(after_v[...], out_buf[...]).astype(BF)
        get_proj.wait()
        get_probs.wait()
        for h in range(HEADS):
            at = [slice(j * HD + h * HEAD, j * HD + (h + 1) * HEAD) for j in range(3)]
            q, k, v = (proj_v[:, a] for a in at)
            grad = gatt_v[:, at[0]]
            half = probs_v[h]
            wide = half.astype(F32)
            gproj_v[:, at[2]] = mm_at(half, grad).astype(BF)
            grad_probs = mm_bt(grad, v)
            spread = grad_probs - jnp.sum(grad_probs * wide, -1, keepdims=True)
            grad_scores = (wide * spread * SCALE).astype(BF)
            gproj_v[:, at[0]] = mm(grad_scores, k).astype(BF)
            gproj_v[:, at[1]] = mm_at(grad_scores, q).astype(BF)
        put_gproj = pltpu.make_async_copy(gproj_v, gproj_o, sems.at[7])
        put_gproj.start()
        for j in range(3):
            weights.wait_third(j)
            part = mm_bt(gproj_v[:, j * HD : (j + 1) * HD], qkv_buf[j].reshape(-1, HD))
            if j == 0:
                acc[...] = part
            else:
                acc[...] += part
        get_normed.wait()
        get_inv.wait()
        wide = normed_v[...].astype(F32)
        mean = jnp.mean(acc[...] * wide, -1, keepdims=True)
        through = inv_v[:, :1] * (acc[...] - normed_v[...].astype(F32) * mean)
        gv[...] = (after_v[...].astype(F32) + through).astype(BF)
        put_gprev = pltpu.make_async_copy(gv, gprev_o, sems.at[8])
        put_gprev.start()
        put_gprev.wait()
        put_after.wait()
        put_gproj.wait()


def backward_section(flag, grad_next, gctl, weights, saved, state, deps):
    rows, width = gctl.shape
    owners, packed = weights
    shards, qkv_rows = (len(packed), width // len(packed))
    tail = [] if grad_next is None else [grad_next]
    normed, inv, proj, probs = saved
    args = (flag, owners, *tail, *packed, gctl, normed, inv, proj, probs, *state, *deps)
    first = 7 + len(tail) + shards
    full = pltpu.VMEM((rows, width), BF)
    return call(
        functools.partial(backward_kernel, bool(tail), shards, len(deps)),
        [jax.ShapeDtypeStruct(s.shape, s.dtype) for s in state],
        [ANY, HBM, HBM],
        [
            full,
            full,
            pltpu.VMEM((3, shards, qkv_rows, HD), BF),
            pltpu.VMEM((HD, width), BF),
            full,
            pltpu.VMEM(inv.shape, F32),
            pltpu.VMEM(proj.shape, BF),
            pltpu.VMEM(probs.shape, BF),
            pltpu.VMEM((rows, HD), BF),
            full,
            pltpu.VMEM(proj.shape, BF),
            pltpu.VMEM((rows, width), F32),
            pltpu.SemaphoreType.DMA((9,)),
            pltpu.SemaphoreType.DMA((4,)),
        ],
        args,
        [SMEM, SMEM] + [ANY] * len(tail) + [HBM] * (5 + shards) + [ANY] + [HBM] * 2 + [ANY] * len(deps),
        {first + i: i for i in range(1, len(state))},
    )


def out_value_kernel(att, after, after_sib, norm, gproj, gproj_sib, *refs):
    low, high = refs[-2:]
    owners, rows, cols = (low.shape[0] * 2, low.shape[1] // 2, low.shape[2])
    clip = after.shape[0]
    values = slice(2 * HD, 3 * HD)
    out = mm(att[:, :clip], after[...]) + mm(att[:, clip:], after_sib[...])
    value = mm(norm[:, :clip], gproj[:, values]) + mm(norm[:, clip:], gproj_sib[:, values])
    for p in range(owners):
        to, at = ((low, p) if p < owners // 2 else (high, p - owners // 2))
        to[at, :rows] = out[p * rows : (p + 1) * rows].astype(BF)
        first = 2 * p * rows
        to[at, rows:, :HD] = value[first : first + rows].astype(BF)
        to[at, rows:, HD:] = value[first + rows : first + 2 * rows].astype(BF)


def product_kernel(norm, gproj, gproj_sib, low, high):
    owners, rows, cols = (low.shape[0] * 2, low.shape[1], low.shape[2])
    clip = gproj.shape[0]
    for p in range(owners):
        to, at = ((low, p) if p < owners // 2 else (high, p - owners // 2))
        mine = norm[p * rows : (p + 1) * rows, :clip]
        other = norm[p * rows : (p + 1) * rows, clip:]
        total = mm(mine, gproj[:, :cols]) + mm(other, gproj_sib[:, :cols])
        to[at] = total.astype(BF)


def owner_products(kernel, args, owners, rows, cols, deps=()):
    vmem = pl.BlockSpec(memory_space=pltpu.VMEM)
    block = jax.ShapeDtypeStruct((owners // 2, rows, cols), BF)
    return pl.pallas_call(
        kernel,
        out_shape=[block, block],
        in_specs=[vmem] * len(args) + [ANY] * len(deps),
        compiler_params=pltpu.CompilerParams(vmem_limit_bytes=32 * MIB),
        cost_estimate=NO_COST,
    )(*args, *deps)


def after_kernel(value, done, out):
    pass


def held_until(value, done):
    return pl.pallas_call(
        after_kernel,
        out_shape=jax.ShapeDtypeStruct(value.shape, value.dtype),
        in_specs=[ANY] * 2,
        out_specs=ANY,
        input_output_aliases={0: 0},
        compiler_params=pltpu.CompilerParams(vmem_limit_bytes=MIB),
        cost_estimate=NO_COST,
    )(value, done)


def owner_kernel(owners, *refs):
    count = owners.shape[0]
    kinds = len(refs) // 4
    for i in range(kinds):
        factor, sib_factor, out, across = refs[i::kinds]
        clip = factor.shape[0]
        rows = out.shape[0] // count
        across[:, :clip] = factor[...].T
        across[:, clip:] = sib_factor[...].T
        for p in range(count):
            start = pl.multiple_of(owners[p] * rows, 16)
            out[p * rows : (p + 1) * rows, :] = across[pl.ds(start, rows), :]


def owner_blocks(factors, sib_factors, bits):
    mine = lax.axis_index("dp")
    flips = [
        [
            sum(1 << bit for i, bit in enumerate(phase_bits(bits, core)) if p >> (bits - 1 - i) & 1)
            for p in range(1 << bits)
        ]
        for core in (0, 1)
    ]
    owners = mine ^ jnp.where(mine % 2 == 0, jnp.array(flips[0]), jnp.array(flips[1]))
    clip = factors[0].shape[0]
    vmem = pl.BlockSpec(memory_space=pltpu.VMEM)
    return pl.pallas_call(
        owner_kernel,
        out_shape=[jax.ShapeDtypeStruct((f.shape[1] // 2, 2 * clip), BF) for f in factors],
        in_specs=[SMEM] + [vmem] * (2 * len(factors)),
        out_specs=[vmem] * len(factors),
        scratch_shapes=[pltpu.VMEM((f.shape[1], 2 * clip), BF) for f in factors],
        compiler_params=pltpu.CompilerParams(vmem_limit_bytes=16 * MIB),
        cost_estimate=NO_COST,
    )(owners.astype(jnp.int32), *factors, *sib_factors)


def sum_phase(low, high, bits, phase):
    arrived = lax.ppermute(high, "dp", phase_pairs(bits, phase))
    if phase + 1 == bits:
        return (low[0].astype(F32) + arrived[0].astype(F32), None)
    count = low.shape[0] // 2
    high = (low[count:].astype(F32) + arrived[count:].astype(F32)).astype(BF)
    return ((low[:count].astype(F32) + arrived[:count].astype(F32)).astype(BF), high)


def sum_to_owner(low, high, bits, factor, done=0):
    for phase in range(done, bits):
        low, high = sum_phase(low, high, bits, phase)
    return low * factor


def shards(
    control_in,
    base_in,
    base_update,
    out_gain,
    cotangent,
    w_qkv,
    w_out,
    w_hint,
    window_offset,
    tile_mask,
    token_layout,
):
    segments = lax.axis_size("segment")
    devices = lax.axis_size("dp")
    mine = lax.axis_index("segment")
    rows, width = control_in.shape
    feat = base_in.shape[1]
    qkv_rows, out_rows = (w_qkv.shape[1], w_out.shape[1])
    factor = float(rows * devices) ** (-0.5)
    bits = (devices // 2).bit_length() - 1
    bias = token_bias(window_offset[0], tile_mask[0], token_layout[0])
    packed, owners, bias = gather_shards(pack_shard(w_qkv[0], w_out[0]), bits, bias)
    last = devices // 2 - 1
    hint_shard, packed[last] = lax.optimization_barrier((w_hint[0], packed[last]))
    weight_hint = lax.all_gather(hint_shard, "dp", axis=0, tiled=True)
    weights = (owners, packed)
    flags = [jnp.where(mine == t, 1, 0).astype(jnp.int32).reshape(1) for t in range(segments)]

    state = unwritten(
        ((rows, width), BF),
        ((rows, HEAD), F32),
        ((rows, 3 * HD), BF),
        ((HEADS, rows, rows), BF),
        ((rows, HD), BF),
        ((rows, width), BF),
    )
    half = rows // 2
    moving = [base_in[:half], base_in[half:]]
    arriving, deps = (control_in, [])

    def hint_of(t, after=()):
        return hint_term(flags[t], base_update[0], state[5], weight_hint, after)

    def sum_passed(t, moving, terms):
        sums = [add_rows(m, term) for m, term in zip(moving, terms)]
        return sums, [lax.ppermute(m, "segment", [(t, t + 1)]) for m in sums]

    terms = None
    for t in range(segments):
        if t > 1:
            deps, moving = sum_passed(t - 1, moving, terms or hint_of(t - 1))
            terms = None
        state, send = forward_section(flags[t], arriving, weights, bias, state, deps)
        if t + 1 < segments:
            arriving = lax.ppermute(send, "segment", [(t, t + 1)])
        if t == 1:
            first_terms = hint_of(0, (arriving,))
            terms = hint_of(1, (arriving,))
            upper = add_rows(moving[0], first_terms[0])
            upper = lax.ppermute(upper, "segment", [(0, 1)])
            lower = add_rows(moving[1], first_terms[1], (upper, terms[0]))
            moving = [upper, lax.ppermute(lower, "segment", [(0, 1)])]
    last = segments - 1
    summed = [
        add_rows(m, term)
        for m, term in zip(moving, terms or hint_of(last))
    ]
    normed, inv, proj, probs, att, ctl = state

    top = unwritten(((rows, feat), F32), ((rows, feat), BF), ((rows, width), BF))
    back = unwritten(((rows, width), BF), ((rows, width), BF), ((rows, 3 * HD), BF))
    gain = out_gain[None]
    owners = devices // 2
    saved = (normed, inv, proj, probs)
    grad_next, deps = (None, [])
    for t in range(segments):
        s = segments - 1 - t
        held = []
        below = [lax.ppermute(m, "segment", [(s, s - 1)]) for m in summed] if s else None
        if t < segments - 1:
            top = top_section(flags[s], summed, cotangent, gain, weight_hint, top, deps)
        if s == 1:
            deps = [] if grad_next is None else [grad_next]
            top = top_section(flags[0], below, cotangent, gain, weight_hint, top, deps)
            factors, _ = lax.optimization_barrier(((normed, att, ctl), top[1]))
            norm_rows, att_rows, ctl_rows = owner_blocks(
                factors, [sibling(f) for f in factors], bits
            )
            hint = owner_products(
                product_kernel, (ctl_rows, top[1], sibling(top[1])), owners, qkv_rows, feat
            )
        if s == 0:
            held = hint[1:]
        back = backward_section(flags[s], grad_next, top[2], weights, saved, back, held)
        deps = [back[2]]
        if s:
            grad_next = lax.ppermute(back[0], "segment", [(s, s - 1)])
        summed = [held_until(b, back[1]) for b in below] if t and s > 1 else below
    _, after, gproj = back
    after_sib, gproj_sib = (sibling(after), sibling(gproj))
    done = min(1, bits - 1)
    if done:
        hint = sum_phase(*hint, bits, 0)
    first = owner_products(
        out_value_kernel,
        (att_rows, after, after_sib, norm_rows, gproj, gproj_sib),
        owners,
        2 * out_rows,
        width,
        hint[1:],
    )
    second = owner_products(
        product_kernel, (norm_rows, gproj, gproj_sib), owners, qkv_rows, 2 * HD
    )
    first = sum_to_owner(*first, bits, factor)
    second = sum_to_owner(*second, bits, factor)
    third = sum_to_owner(*hint, bits, factor, done)
    value = jnp.concatenate((first[out_rows:, :HD], first[out_rows:, HD:]), 0)
    return (
        top[0],
        jnp.concatenate((second, value), 1)[None],
        first[None, :out_rows],
        third[None],
    )


def solution(mesh):
    placed = (
        P("dp", None),
        P("dp", None),
        P("segment", "dp", None),
        P(),
        P("dp", None),
        P("segment", "dp", None),
        P("segment", "dp", None),
        P("segment", "dp", None),
        P("segment", None),
        P("segment", None, None),
        P("dp", None),
    )
    return jax.shard_map(
        shards,
        mesh=mesh,
        in_specs=placed,
        out_specs=(
            P("dp", None),
            P("segment", "dp", None),
            P("segment", "dp", None),
            P("segment", "dp", None),
        ),
        check_vma=False,
    )
```
